256 devices in a mesh: plane: 8 (over z_hi, core), ray: 32 (over x, y, z_lo).
Axes of the slice: x: 4, y: 4, z: 8 (z_hi: 4, z_lo: 2; z = z_hi * 2 + z_lo), core: 2. Of those that a mesh axis runs over, the one named last changes fastest.
Arguments:
- kappa: bfloat16 [2, 256, 16384], P(None, 'plane', 'ray'), may hold values from 0.049804688 to 2
- row_kernel: float32 [4, 63], replicated, may hold values from -0.75 to 0.75
- col_kernel: float32 [4, 63], replicated, may hold values from -0.75 to 0.75
- positions: float32 [2, 1048576], P(None, ('plane', 'ray')), may hold values from -6 to 6
- cells: int32 [2, 1048576], P(None, ('plane', 'ray')), may hold values from 0 to 131071
- owners: int32 [2, 8192, 1], P(None, ('plane', 'ray')), may hold values from 0 to 31; in each aligned block of 32 rows (0 to 31, 32 to 63, ..., all dimensions but the last counted through in order) at most 2 rows name the same one
- counts: int32 [256], P(('plane', 'ray')), may hold values from 24 to 32, as said below
Outputs:
- final_positions: float32 [2, 1048576], P(None, ('plane', 'ray'))
- jacobian: float32 [4, 1048576], P(None, ('plane', 'ray'))
The draws below stay inside these ranges and needn't reach their ends.
Inputs may be any that keep to these rules, and one draw needn't show every extreme that they name: `owners`: in each aligned run of 32 blocks of one plane no tile is named by more than 2 blocks, a bound that some block reaches. `counts`: some group has all 32 blocks traced and some group exactly 24.
All inputs are finite; a program needn't handle non-finite values.
Results may differ from the reference program's by a relative error of at most 0.0023.
Values may be sent and summed in bfloat16 or wider, within the bound.
A program may use at most 320 MiB of HBM per device.

```python
import math
import jax
import jax.numpy as jnp
import numpy as np

COLS = 512
TAPS = 63
NB = 32
BLOCK = 128
CAP = 2
TILE_ROWS = 256
SLAB_COLS = 16384
BLOCKS = 8192
RAYS = 1048576
N_RAY = 32
DEVICES = 256


def draw_counts(key, part):
    lowest = 3 * NB // 4
    values = jax.random.randint(key, (DEVICES,), lowest, NB + 1)
    first = jax.random.randint(jax.random.fold_in(key, 1), (), 0, DEVICES)
    stride = jax.random.randint(jax.random.fold_in(key, 2), (), 1, DEVICES)
    second = (first + stride) % DEVICES
    values = values.at[first].set(NB)
    values = values.at[second].set(lowest)
    return values.astype(jnp.int32)


def plant(values, stream_key, low, largest):
    longest = values.shape.index(max(values.shape))
    spots = []
    for shift in (0, 1):
        where = [jax.random.randint(jax.random.fold_in(stream_key, axis), (), 0, length) for axis, length in enumerate(values.shape)]
        where[longest] = (where[longest] + shift) % values.shape[longest]
        spots.append(tuple(where))
    return values.at[spots[0]].set(low).at[spots[1]].set(largest)


def level_of(key, extent, split, least, high):
    def one(position, parts):
        heights = jax.random.uniform(jax.random.fold_in(jax.random.fold_in(key, 6), position), (parts,), jnp.float32, least / len(split), high / len(split))
        return jnp.repeat(jnp.exp(heights), extent[position] // parts).reshape((-1,) + (1,) * (len(extent) - position - 1))

    level = one(*split[0])
    for cut in split[1:]:
        level = level * one(*cut)
    return level


def shared_out(stream_key, own, number, rows, count, top, most, slope):
    ranking = jax.random.permutation(stream_key, count)
    crowded, common = shares(count, rows * top, most, slope, True), shares(count, rows * top, most, slope, False)
    places = jnp.arange(count)

    def named(lengths, offset_by):
        used = int((lengths > 0).sum())
        fixed = max(1, used // 4)
        passed = fixed + (places - fixed + offset_by * (used - fixed)) % max(1, count - fixed)
        return jnp.zeros((count,), jnp.int32).at[ranking[jnp.where(places < fixed, places, passed)]].set(jnp.asarray(lengths, jnp.int32))

    lengths = jnp.where(number % 4 == 0, named(crowded, number // 4), named(common, number - number // 4 - 1))
    mixed = jax.random.permutation(jax.random.fold_in(own, 3), count)
    giver, sink = mixed[0:count // 2 * 2:2], mixed[1:count // 2 * 2:2]
    room = jnp.minimum(lengths[giver] - 1, most - lengths[sink]) // 2
    room = jnp.where((giver == ranking[0]) | (sink == ranking[0]) | (lengths[sink] == 0), 0, jnp.maximum(room, 0))
    passed = jax.random.randint(jax.random.fold_in(own, 4), (count // 2,), 0, 1 << 20) % (room + 1)
    lengths = lengths.at[giver].add(-passed).at[sink].add(passed)
    labels = jnp.searchsorted(jnp.cumsum(lengths), jnp.arange(rows * top), side="right").astype(jnp.int32)
    listing = labels.reshape(top, rows).T
    listing = listing[jax.random.permutation(jax.random.fold_in(own, 1), rows)]
    offset_by = jax.random.randint(jax.random.fold_in(own, 2), (rows, 1), 0, top)
    return jnp.take_along_axis(listing, (jnp.arange(top)[None, :] + offset_by) % top, axis=1)


def shares(number_of, total, bound, lean, full):
    loads = [(1 << 20) // math.isqrt(rank ** lean) + 1 for rank in range(1, number_of + 1)]
    largest = bound if full else min(bound, max(-(-total // number_of), total * loads[0] // sum(loads)))
    least = 1 if total - largest >= number_of - 1 else 0
    holding, rest = [largest] + [least] * (number_of - 1), total - largest - least * (number_of - 1)
    while rest > 0:
        candidates = [i for i in range(1, number_of) if holding[i] < largest] or [i for i in range(1, number_of) if holding[i] < bound]
        pool, left = sum([loads[i] for i in candidates]), rest
        for i in candidates:
            more = min(bound - holding[i], max(1, left * loads[i] // pool), rest)
            holding[i] = holding[i] + more
            rest = rest - more
    return np.array(holding)


def bell_draw(key, extent, width, reach, cuts=(), kind=jnp.bfloat16):
    values = jax.random.normal(key, extent, jnp.float32) * width
    if len(cuts) > 0:
        values = level_of(key, extent, cuts, -0.22, 0.18) * values
    return jnp.clip(values, min=-reach, max=reach).astype(kind)


def setup_inputs(seed: int = 0) -> dict:
    key_of = jax.random.split(jax.random.key(seed), 8)
    kappa = jnp.clip(jnp.exp(math.log(2.0) - 3.6927934 * jax.random.uniform(key_of[0], (2, TILE_ROWS, SLAB_COLS), jnp.float32) ** level_of(key_of[0], (2, TILE_ROWS, SLAB_COLS), ((1, 8), (2, 32)), -0.2, 0.2)), 0.049804688, 2.0).astype(jnp.bfloat16)
    row_kernel = bell_draw(key_of[1], (4, TAPS), TAPS ** -0.5, 0.75, (), jnp.float32)
    col_kernel = bell_draw(key_of[2], (4, TAPS), TAPS ** -0.5, 0.75, (), jnp.float32)
    positions = bell_draw(key_of[3], (2, RAYS), 1.0, 6.0, ((1, 256),), jnp.float32)
    cells = plant(jax.random.randint(key_of[4], (2, RAYS), 0, TILE_ROWS * COLS), jax.random.fold_in(key_of[4], 1), 0, (TILE_ROWS * COLS) - 1).astype(jnp.int32)
    owners_keys = jax.random.split(jax.random.fold_in(key_of[5], 1), 2 * BLOCKS // NB)
    owners_turns = jax.random.permutation(jax.random.fold_in(key_of[5], 3), 2 * BLOCKS // NB)
    owners = jax.vmap(lambda own, number: shared_out(jax.random.fold_in(key_of[5], 2), own, number, NB, N_RAY, 1, CAP, 2))(owners_keys, owners_turns).reshape((2, BLOCKS, 1))
    counts = draw_counts(jax.random.fold_in(key_of[7], 71), 0)
    return {"kappa": kappa, "row_kernel": row_kernel, "col_kernel": col_kernel, "positions": positions, "cells": cells, "owners": owners, "counts": counts}


lens_weights = (0.6, 0.4)


def advance(ray_state, samples, plane_weight):
    pos_x, pos_y, jac_xx, jac_xy, jac_yx, jac_yy = ray_state
    deflect_x, deflect_y, shear_one, shear_two, converge = samples
    mat_xx = converge + shear_one
    mat_yy = converge - shear_one
    mat_xy = shear_two
    return (pos_x - plane_weight * deflect_x,
            pos_y - plane_weight * deflect_y,
            jac_xx - plane_weight * (mat_xx * jac_xx + mat_xy * jac_yx),
            jac_xy - plane_weight * (mat_xx * jac_xy + mat_xy * jac_yy),
            jac_yx - plane_weight * (mat_xy * jac_xx + mat_yy * jac_yx),
            jac_yy - plane_weight * (mat_xy * jac_xy + mat_yy * jac_yy))


def conv_fields(kappa, row_kernel, col_kernel):
    tap_count = row_kernel.shape[1]
    margin = (tap_count - 1) // 2
    base = kappa.astype(jnp.float32)
    padded = jnp.pad(base, ((0, 0), (margin, margin), (margin, margin)))
    row_count = base.shape[1]
    col_count = base.shape[2]
    channels = []
    for channel in range(4):
        column_pass = jnp.zeros((base.shape[0], row_count + 2 * margin, col_count), jnp.float32)
        for tap_id in range(tap_count):
            column_pass = column_pass + col_kernel[channel, tap_id] * padded[:, :, tap_id:tap_id + col_count]
        row_pass = jnp.zeros((base.shape[0], row_count, col_count), jnp.float32)
        for tap_id in range(tap_count):
            row_pass = row_pass + row_kernel[channel, tap_id] * column_pass[:, tap_id:tap_id + row_count, :]
        channels.append(row_pass)
    convolved = jnp.stack(channels, axis=1).astype(jnp.bfloat16)
    return jnp.concatenate([convolved, kappa[:, None]], axis=1)


def reference(kappa, row_kernel, col_kernel, positions, cells, owners, counts):
    field_stack = conv_fields(kappa, row_kernel, col_kernel)
    ray_total = positions.shape[1]
    ray_ids = jnp.arange(ray_total, dtype=jnp.int32)
    block_ids = ray_ids // BLOCK
    traced = (block_ids % NB) < counts[block_ids // NB]
    ones_row = jnp.ones((ray_total,), jnp.float32)
    zeros_row = jnp.zeros((ray_total,), jnp.float32)
    ray_state = (positions[0], positions[1], ones_row, zeros_row, zeros_row, ones_row)
    for plane_id in range(2):
        targets = owners[plane_id, :, 0][block_ids]
        cell_rows = cells[plane_id] // COLS
        cell_columns = targets * COLS + cells[plane_id] % COLS
        samples = field_stack[plane_id][:, cell_rows, cell_columns].astype(jnp.float32)
        ray_state = advance(ray_state, [samples[member] for member in range(5)], lens_weights[plane_id])
    start = (positions[0], positions[1], ones_row, zeros_row, zeros_row, ones_row)
    result = [jnp.where(traced, ray_state[member], start[member]) for member in range(6)]
    return jnp.stack(result[:2], axis=0), jnp.stack(result[2:], axis=0)
```

```python
import functools
import jax
import jax.numpy as jnp
from jax import lax
from jax.experimental import pallas as pl
from jax.experimental.pallas import tpu as pltpu
from jax.sharding import PartitionSpec as P

MESH = pl.DeviceIdType.MESH
LENS_WEIGHTS = (0.6, 0.4)
CHANNELS = 5
EDGE = 128
WIDE = 384
F32 = jnp.float32
BF16 = jnp.bfloat16


def iota(shape, dim):
    return lax.broadcasted_iota(jnp.int32, shape, dim)


def mod(a, b):
    return lax.rem(a, b)


def split(x):
    high = x.astype(BF16)
    return high, (x - high.astype(F32)).astype(BF16)


def dot(a, b):
    return jnp.dot(a, b, preferred_element_type=F32)


def dot_t(a, b):
    return lax.dot_general(a, b, (((1,), (1,)), ((), ())), preferred_element_type=F32)


def advance(ray_state, samples, plane_weight):
    pos_x, pos_y, jac_xx, jac_xy, jac_yx, jac_yy = ray_state
    deflect_x, deflect_y, shear_one, shear_two, converge = samples
    mat_xx = converge + shear_one
    mat_yy = converge - shear_one
    return (
        pos_x - plane_weight * deflect_x,
        pos_y - plane_weight * deflect_y,
        jac_xx - plane_weight * (mat_xx * jac_xx + shear_two * jac_yx),
        jac_xy - plane_weight * (mat_xx * jac_xy + shear_two * jac_yy),
        jac_yx - plane_weight * (shear_two * jac_xx + mat_yy * jac_yx),
        jac_yy - plane_weight * (shear_two * jac_xy + mat_yy * jac_yy),
    )


def kernel(
    planes, tiles,
    kappa, row_kernel, col_kernel, positions, cells, owners, counts,
    final, jacobian,
    slab, taps, col_high, col_low, row_high, row_low, pass_high, pass_low, table,
    start_xy, cell_rows, cell_out, cell_in, stage, found, samples,
    kappa_send, kappa_recv, cell_send, cell_recv, found_send, found_recv,
):
    p, r = lax.axis_index("plane"), lax.axis_index("ray")
    k = mod(p, 2)
    base = p - k
    own_rows = kappa.shape[1]
    cols = kappa.shape[2]
    rows = planes * own_rows
    blocks = owners.shape[2]
    peers = 2 * tiles
    margin = (row_kernel.shape[1] - 1) // 2

    def peer(u):
        return mod(k + u, 2), mod(r + u // 2, tiles)

    def column_mate(e, w):
        return mod(base + 2 * e, planes) + mod(k + w, 2)

    others = [(e, w) for e in range(1, planes // 2) for w in range(2)]

    barrier = pltpu.get_barrier_semaphore()

    def greet(dp, dr):
        pl.semaphore_signal(barrier, inc=1, device_id=(dp, dr), device_id_type=MESH)

    @pl.loop(1, peers)
    def _(u):
        kk, t = peer(u)
        greet(base + kk, t)

    for e, w in others:
        dp = column_mate(e, w)
        greet(dp, r)

        @pl.when(r > 0)
        def _():
            greet(dp, r - 1)

        @pl.when(r < tiles - 1)
        def _():
            greet(dp, r + 1)

    for b in range(blocks):
        lanes = pl.ds(b * 128, 128)
        for m in range(2):
            start_xy[m, b : b + 1, :] = positions[m : m + 1, lanes]
            cell_rows[m, b : b + 1, :] = cells[m : m + 1, lanes]
    left_id = iota((blocks, blocks), 0)
    right_id = iota((blocks, blocks), 1)
    traced_row = iota((1, blocks), 1) < counts[0]
    traced_col = iota((blocks, 1), 0) < counts[0]
    target_cols = []
    for m in range(2):
        owner_row = owners[m]
        owner_col = jnp.sum(
            jnp.where(left_id == right_id, jnp.broadcast_to(owner_row, (blocks, blocks)), 0),
            axis=1, keepdims=True,
        )
        same = owner_col == owner_row
        slot_row = jnp.sum((same & (left_id < right_id)).astype(jnp.int32), axis=0, keepdims=True)
        slot_col = jnp.sum((same & (right_id < left_id)).astype(jnp.int32), axis=1, keepdims=True)
        dest_row = jnp.where(traced_row, owner_row * 2 + slot_row, -1)
        target_cols.append(jnp.where(traced_col, owner_col * 2 + slot_col, -1))
        choose = (iota((peers, blocks), 0) == dest_row).astype(F32).astype(BF16)
        ids = cell_rows[m]
        pieces = jnp.concatenate(
            [(ids >> 9).astype(F32), ((ids >> 8) & 1).astype(F32), (ids & 255).astype(F32)], axis=1
        ).astype(BF16)
        sent = dot(choose, pieces).astype(jnp.int32)
        out = sent[:, :128] * 512 + sent[:, 128:256] * 256 + sent[:, 256:]
        for t in range(tiles):
            cell_out[m, t, :, 0:128] = out[2 * t : 2 * t + 1]
            cell_out[m, t, :, 128:256] = out[2 * t + 1 : 2 * t + 2]

    sides = jnp.minimum(r, 1) + jnp.minimum(tiles - 1 - r, 1)
    pl.semaphore_wait(barrier, peers - 1 + len(others) * (1 + sides))

    def remote(src, dst, send_sem, recv_sem, dp, dr):
        return pltpu.make_async_remote_copy(
            src_ref=src, dst_ref=dst, send_sem=send_sem, recv_sem=recv_sem,
            device_id=(dp, dr), device_id_type=MESH,
        )

    order = [(e, w) for e in sorted(range(planes // 2), key=lambda e: -min(e, planes // 2 - e)) for w in (1, 0)]

    def slab_part(q, d):
        lanes = (pl.ds(EDGE, cols), pl.ds(0, EDGE), pl.ds(EDGE + cols, EDGE))[d]
        return slab.at[pl.ds(q * own_rows, own_rows), lanes]

    def kappa_part(m, d):
        lanes = (pl.ds(0, cols), pl.ds(cols - EDGE, EDGE), pl.ds(0, EDGE))[d]
        return kappa.at[m, :, lanes]

    def kappa_copy(e, w, d, sender):
        dp = column_mate(e, w)
        dr = (r, r + 1, r - 1)[d]
        return remote(
            kappa_part(mod(k + w, 2), d), slab_part(sender, d),
            kappa_send.at[e, w, d], kappa_recv.at[sender, d], dp, dr,
        )

    for e, w in order:
        if (e, w) != (0, 0):
            kappa_copy(e, w, 0, p).start()
    for e, w in order:

        @pl.when(r < tiles - 1)
        def _():
            kappa_copy(e, w, 1, p).start()

        @pl.when(r > 0)
        def _():
            kappa_copy(e, w, 2, p).start()

    def cell_copy(u):
        kk, t = peer(u)
        return remote(
            cell_out.at[kk, t], cell_in.at[k, r], cell_send.at[u], cell_recv.at[k, r], base + kk, t
        )

    def cell_arrival(u):
        kk, t = peer(u)
        return remote(
            cell_out.at[kk, t], cell_in.at[kk, t], cell_send.at[u], cell_recv.at[kk, t], base + kk, t
        )

    @pl.loop(1, peers)
    def _(u):
        cell_copy(u).start()

    cell_in[k, r] = cell_out[k, r]
    slab[pl.ds(p * own_rows, own_rows), EDGE : EDGE + cols] = kappa[k]

    @pl.when(r == 0)
    def _():
        slab[:, 0:EDGE] = jnp.zeros((rows, EDGE), BF16)

    @pl.when(r == tiles - 1)
    def _():
        slab[:, EDGE + cols :] = jnp.zeros((rows, EDGE), BF16)

    taps[...] = jnp.zeros_like(taps)
    taps[0:4, 0 : row_kernel.shape[1]] = row_kernel[...]
    taps[4:8, 0 : row_kernel.shape[1]] = col_kernel[...]
    for c in range(4):
        across = jnp.broadcast_to(taps[4 + c : 5 + c, :], (EDGE, WIDE))
        band = pltpu.roll(across, EDGE - margin, 1, stride=1, stride_axis=0)
        col_high[c * EDGE : (c + 1) * EDGE, :], col_low[c * EDGE : (c + 1) * EDGE, :] = split(band)
        down = jnp.broadcast_to(taps[c : c + 1, :], (rows, WIDE))
        band = pltpu.roll(down, WIDE - margin, 1, stride=1, stride_axis=0)[:, :rows]
        row_high[c], row_low[c] = split(band)
    stage[...] = jnp.zeros_like(stage)

    for e, w in order:
        if (e, w) != (0, 0):
            kappa_copy(e, w, 0, column_mate(e, w)).wait_recv()
    for e, w in order:

        @pl.when(r < tiles - 1)
        def _():
            kappa_copy(e, w, 2, column_mate(e, w)).wait_recv()

        @pl.when(r > 0)
        def _():
            kappa_copy(e, w, 1, column_mate(e, w)).wait_recv()

    for j in range(cols // EDGE):
        window = slab[:, j * EDGE : j * EDGE + WIDE]
        passed = dot_t(window, col_high[...]) + dot_t(window, col_low[...])
        for c in range(4):
            lanes = slice(j * EDGE, (j + 1) * EDGE)
            pass_high[c, :, lanes], pass_low[c, :, lanes] = split(passed[:, c * EDGE : (c + 1) * EDGE])
    for c in range(4):
        field = (
            dot(row_high[c], pass_high[c]) + dot(row_low[c], pass_high[c]) + dot(row_high[c], pass_low[c])
        )
        table[c * rows : (c + 1) * rows, :] = field.astype(BF16)
    table[4 * rows :, :] = slab[:, EDGE : EDGE + cols]

    @pl.loop(1, peers)
    def _(u):
        cell_arrival(u).wait_recv()

    def look_up(u):
        kk, t = peer(u)
        ids = cell_in[kk, t]
        hot = (iota((cols, 256), 0) == (ids & (cols - 1))).astype(F32).astype(BF16)
        picked = dot(table[...], hot)
        mine = iota((rows, 256), 0) == (ids >> 9)
        for c in range(CHANNELS):
            value = jnp.sum(jnp.where(mine, picked[c * rows : (c + 1) * rows], 0.0), axis=0, keepdims=True)
            stage[c : c + 1, :] = value[:, :128]
            stage[8 + c : 9 + c, :] = value[:, 128:]
        return stage[...].astype(BF16)

    def found_copy(u):
        kk, t = peer(u)
        return remote(
            found.at[u], samples.at[k, r], found_send.at[u], found_recv.at[k, r], base + kk, t
        )

    def found_arrival(u):
        kk, t = peer(u)
        return remote(
            found.at[u], samples.at[kk, t], found_send.at[u], found_recv.at[kk, t], base + kk, t
        )

    @pl.loop(1, peers)
    def _(u):
        found[u] = look_up(u)
        found_copy(u).start()

    samples[k, r] = look_up(0)

    @pl.loop(1, peers)
    def _(u):
        found_arrival(u).wait_recv()

    initial = (start_xy[0], start_xy[1], 1.0, 0.0, 0.0, 1.0)
    state = (start_xy[0], start_xy[1]) + tuple(
        jnp.full((blocks, 128), v, F32) for v in initial[2:]
    )
    for m in range(2):
        target = jnp.concatenate([target_cols[m] * 8 + c for c in range(CHANNELS)], axis=0)
        wanted = (iota((CHANNELS * blocks, tiles * 16), 1) == target).astype(F32).astype(BF16)
        got = dot(wanted, samples[m].reshape(tiles * 16, 128))
        state = advance(
            state, [got[c * blocks : (c + 1) * blocks] for c in range(CHANNELS)], LENS_WEIGHTS[m]
        )
    for v in range(6):
        value = jnp.where(traced_col, state[v], initial[v])
        ref, row = (final, v) if v < 2 else (jacobian, v - 2)
        for b in range(blocks):
            ref[row : row + 1, b * 128 : (b + 1) * 128] = value[b : b + 1]

    for e, w in order:
        if (e, w) != (0, 0):
            kappa_copy(e, w, 0, p).wait_send()
    for e, w in order:

        @pl.when(r < tiles - 1)
        def _():
            kappa_copy(e, w, 1, p).wait_send()

        @pl.when(r > 0)
        def _():
            kappa_copy(e, w, 2, p).wait_send()

    @pl.loop(1, peers)
    def _(u):
        cell_copy(u).wait_send()
        found_copy(u).wait_send()


def local(planes, tiles, kappa, row_kernel, col_kernel, positions, cells, owners, counts):
    own_rows, cols = kappa.shape[1:]
    rows = planes * own_rows
    blocks = owners.shape[1]
    rays = positions.shape[1]
    peers = 2 * tiles
    in_vmem = pl.BlockSpec(memory_space=pltpu.VMEM)
    dma = pltpu.SemaphoreType.DMA
    return pl.pallas_call(
        functools.partial(kernel, planes, tiles),
        out_shape=(
            jax.ShapeDtypeStruct((2, rays), F32),
            jax.ShapeDtypeStruct((4, rays), F32),
        ),
        in_specs=[in_vmem] * 6 + [pl.BlockSpec(memory_space=pltpu.SMEM)],
        out_specs=(in_vmem, in_vmem),
        scratch_shapes=[
            pltpu.VMEM((rows, cols + 2 * EDGE), BF16),
            pltpu.VMEM((8, WIDE), F32),
            pltpu.VMEM((4 * EDGE, WIDE), BF16),
            pltpu.VMEM((4 * EDGE, WIDE), BF16),
            pltpu.VMEM((4, rows, rows), BF16),
            pltpu.VMEM((4, rows, rows), BF16),
            pltpu.VMEM((4, rows, cols), BF16),
            pltpu.VMEM((4, rows, cols), BF16),
            pltpu.VMEM((CHANNELS * rows, cols), BF16),
            pltpu.VMEM((2, blocks, 128), F32),
            pltpu.VMEM((2, blocks, 128), jnp.int32),
            pltpu.VMEM((2, tiles, 1, 256), jnp.int32),
            pltpu.VMEM((2, tiles, 1, 256), jnp.int32),
            pltpu.VMEM((16, 128), F32),
            pltpu.VMEM((peers, 16, 128), BF16),
            pltpu.VMEM((2, tiles, 16, 128), BF16),
            dma((planes // 2, 2, 3)),
            dma((planes, 3)),
            dma((peers,)),
            dma((2, tiles)),
            dma((peers,)),
            dma((2, tiles)),
        ],
        compiler_params=pltpu.CompilerParams(
            collective_id=0, has_side_effects=True, vmem_limit_bytes=48 * 2**20
        ),
    )(kappa, row_kernel, col_kernel, positions, cells, owners.reshape(2, 1, blocks), counts)


def solution(mesh):
    return jax.shard_map(
        functools.partial(local, mesh.shape["plane"], mesh.shape["ray"]),
        mesh=mesh,
        in_specs=(
            P(None, "plane", "ray"),
            P(),
            P(),
            P(None, ("plane", "ray")),
            P(None, ("plane", "ray")),
            P(None, ("plane", "ray"), None),
            P(("plane", "ray")),
        ),
        out_specs=(P(None, ("plane", "ray")), P(None, ("plane", "ray"))),
        check_vma=False,
    )
```

```python
import functools
import jax
import jax.numpy as jnp
from jax import lax
from jax.experimental import pallas as pl
from jax.experimental.pallas import tpu as pltpu
from jax.sharding import PartitionSpec as P

MESH = pl.DeviceIdType.MESH
LENS_WEIGHTS = (0.6, 0.4)
CHANNELS = 5
EDGE = 128
WIDE = 384
GROUP = 8
F32 = jnp.float32
BF16 = jnp.bfloat16


def iota(shape, dim):
    return lax.broadcasted_iota(jnp.int32, shape, dim)


def mod(a, b):
    return lax.rem(a, b)


def split(x):
    high = x.astype(BF16)
    return high, (x - high.astype(F32)).astype(BF16)


def dot(a, b):
    return jnp.dot(a, b, preferred_element_type=F32)


def dot_t(a, b):
    return lax.dot_general(a, b, (((1,), (1,)), ((), ())), preferred_element_type=F32)


def advance(ray_state, samples, plane_weight):
    pos_x, pos_y, jac_xx, jac_xy, jac_yx, jac_yy = ray_state
    deflect_x, deflect_y, shear_one, shear_two, converge = samples
    mat_xx = converge + shear_one
    mat_yy = converge - shear_one
    return (
        pos_x - plane_weight * deflect_x,
        pos_y - plane_weight * deflect_y,
        jac_xx - plane_weight * (mat_xx * jac_xx + shear_two * jac_yx),
        jac_xy - plane_weight * (mat_xx * jac_xy + shear_two * jac_yy),
        jac_yx - plane_weight * (shear_two * jac_xx + mat_yy * jac_yx),
        jac_yy - plane_weight * (shear_two * jac_xy + mat_yy * jac_yy),
    )


def kernel(
    planes, grid,
    kappa_hbm, row_kernel_hbm, col_kernel_hbm, positions_hbm, cells_hbm, owners_hbm, counts,
    final, jacobian,
    row_kernel, col_kernel, positions, cells, owners,
    slab, halo, edge, taps, col_high, col_low, row_high, row_low, pass_high, pass_low, table, rows_of,
    start_xy, cell_rows, cell_out, cell_one, cell_two, cell_in, offsets, offset_of, found, samples,
    load_sem, halo_send, halo_recv, kappa_send, kappa_recv, edge_send, edge_recv,
    cell_send, cell_recv, found_send, found_recv,
):
    tx, ty = grid
    tiles = tx * ty * 2
    p, r = lax.axis_index("plane"), lax.axis_index("ray")
    k = mod(p, 2)
    base = p - k
    x, y, zl = r // (2 * ty), mod(r // 2, ty), mod(r, 2)
    near = zl * 2 + k
    own_rows, cols = kappa_hbm.shape[1:]
    rows = planes * own_rows
    blocks = owners.shape[2]
    peers = 2 * tiles
    margin = (row_kernel.shape[1] - 1) // 2

    def peer(u):
        return mod(k + u, 2), mod(r + u // 2, tiles)

    def near_mate(w):
        q = mod(near + w, 4)
        return q, base + mod(q, 2), r - zl + q // 2

    def y_mate(w):
        yy = mod(y + w, ty)
        return yy, r + 2 * (yy - y)

    def x_mate(w):
        xx = mod(x + w, tx)
        return xx, r + 2 * ty * (xx - x)

    def column_mate(e, w):
        return mod(base + 2 * e, planes) + mod(k + w, 2)

    half = planes // 2
    order = [
        (e, w) for e in sorted(range(half), key=lambda e: -min(e, half - e)) for w in (1, 0) if (e, w) != (0, 0)
    ]
    far = [(e, w) for e, w in order if e]

    barrier = pltpu.get_barrier_semaphore()

    def greet(dp, dr):
        pl.semaphore_signal(barrier, inc=1, device_id=(dp, dr), device_id_type=MESH)

    @pl.when(r > 0)
    def _():
        greet(p, r - 1)

    @pl.when(r < tiles - 1)
    def _():
        greet(p, r + 1)

    for w in range(1, 4):
        greet(*near_mate(w)[1:])
    for e, w in far:
        greet(column_mate(e, w), r)
    for w in range(1, ty):
        greet(p, y_mate(w)[1])
    for w in range(1, tx):
        greet(p, x_mate(w)[1])

    loads = [
        pltpu.make_async_copy(src, dst, load_sem.at[i])
        for i, (src, dst) in enumerate([
            (owners_hbm, owners),
            (cells_hbm, cells),
            (row_kernel_hbm, row_kernel),
            (col_kernel_hbm, col_kernel),
            (positions_hbm, positions),
            (kappa_hbm.at[k], slab.at[pl.ds(p * own_rows, own_rows), pl.ds(EDGE, cols)]),
        ])
    ]
    for load in loads:
        load.start()
    for load in loads[:2]:
        load.wait()

    for b in range(blocks):
        lanes = pl.ds(b * 128, 128)
        for m in range(2):
            cell_rows[m, b : b + 1, :] = cells[m : m + 1, lanes]
    left_id = iota((blocks, blocks), 0)
    right_id = iota((blocks, blocks), 1)
    traced_row = iota((1, blocks), 1) < counts[0]
    traced_col = iota((blocks, 1), 0) < counts[0]
    target_cols = []
    for m in range(2):
        owner_row = owners[m]
        owner_col = jnp.sum(
            jnp.where(left_id == right_id, jnp.broadcast_to(owner_row, (blocks, blocks)), 0),
            axis=1, keepdims=True,
        )
        same = owner_col == owner_row
        slot_row = jnp.sum((same & (left_id < right_id)).astype(jnp.int32), axis=0, keepdims=True)
        slot_col = jnp.sum((same & (right_id < left_id)).astype(jnp.int32), axis=1, keepdims=True)
        dest_row = jnp.where(traced_row, owner_row * 2 + slot_row, -1)
        target_cols.append(jnp.where(traced_col, owner_col * 2 + slot_col, -1))
        choose = (iota((peers, blocks), 0) == dest_row).astype(jnp.int32)
        ids = cell_rows[m]
        out = sum(choose[:, b : b + 1] * ids[b : b + 1] for b in range(blocks))
        for t in range(tiles):
            where = (t % 2 * 2 + m, t // (2 * ty), t // 2 % ty)
            cell_out[where + (slice(None), slice(0, 128))] = out[2 * t : 2 * t + 1]
            cell_out[where + (slice(None), slice(128, 256))] = out[2 * t + 1 : 2 * t + 2]

    sides = jnp.minimum(r, 1) + jnp.minimum(tiles - 1 - r, 1)
    pl.semaphore_wait(barrier, 3 + len(far) + ty - 1 + tx - 1 + sides)

    def remote(src, dst, send_sem, recv_sem, dp, dr):
        return pltpu.make_async_remote_copy(
            src_ref=src, dst_ref=dst, send_sem=send_sem, recv_sem=recv_sem,
            device_id=(dp, dr), device_id_type=MESH,
        )

    def to_right():
        return remote(
            kappa_hbm.at[:, :, pl.ds(cols - EDGE, EDGE)], halo.at[0], halo_send.at[0], halo_recv.at[0], p, r + 1
        )

    def to_left():
        return remote(
            kappa_hbm.at[:, :, pl.ds(0, EDGE)], halo.at[1], halo_send.at[1], halo_recv.at[1], p, r - 1
        )

    def own_part(q, lanes):
        return slab.at[pl.ds(q * own_rows, own_rows), lanes]

    def kappa_copy(e, w, sender):
        return remote(
            kappa_hbm.at[mod(k + w, 2)], own_part(sender, pl.ds(EDGE, cols)),
            kappa_send.at[e, w], kappa_recv.at[sender], column_mate(e, w), r,
        )

    def edge_copy(e, w, sender):
        return remote(
            edge.at[mod(k + w, 2)], own_part(sender, pl.ds(0, EDGE)),
            edge_send.at[e, w], edge_recv.at[sender], column_mate(e, w), r,
        )

    def cell_near(w, arrival):
        q, dp, dr = near_mate(w)
        slot = q if arrival else near
        return remote(cell_out.at[q], cell_one.at[slot], cell_send.at[0, w], cell_recv.at[0, slot], dp, dr)

    def cell_y(w, arrival):
        yy, dr = y_mate(w)
        slot = yy if arrival else y
        return remote(
            cell_one.at[:, :, yy], cell_two.at[slot], cell_send.at[1, w], cell_recv.at[1, slot], p, dr
        )

    def cell_x(w, arrival):
        xx, dr = x_mate(w)
        slot = xx if arrival else x
        return remote(
            cell_two.at[:, :, xx], cell_in.at[slot], cell_send.at[2, w], cell_recv.at[2, slot], p, dr
        )

    @pl.when(r < tiles - 1)
    def _():
        to_right().start()

    @pl.when(r > 0)
    def _():
        to_left().start()

    for w in range(1, 4):
        cell_near(w, False).start()
    for e, w in order:
        kappa_copy(e, w, p).start()
    cell_one[near] = cell_out[near]

    @pl.when(r == 0)
    def _():
        halo[0] = jnp.zeros(halo.shape[1:], BF16)

    @pl.when(r == tiles - 1)
    def _():
        halo[1] = jnp.zeros(halo.shape[1:], BF16)

    for load in loads[2:]:
        load.wait()

    taps[...] = jnp.zeros_like(taps)
    taps[0:4, 0 : row_kernel.shape[1]] = row_kernel[...]
    taps[4:8, 0 : row_kernel.shape[1]] = col_kernel[...]

    def bands(c):
        across = jnp.broadcast_to(taps[4 + c : 5 + c, :], (EDGE, WIDE))
        band = pltpu.roll(across, EDGE - margin, 1, stride=1, stride_axis=0)
        col_high[c * EDGE : (c + 1) * EDGE, :], col_low[c * EDGE : (c + 1) * EDGE, :] = split(band)
        down = jnp.broadcast_to(taps[c : c + 1, :], (rows, WIDE))
        band = pltpu.roll(down, WIDE - margin, 1, stride=1, stride_axis=0)[:, :rows]
        row_high[c], row_low[c] = split(band)

    bands(0)

    @pl.when(r > 0)
    def _():
        to_right().wait_recv()

    @pl.when(r < tiles - 1)
    def _():
        to_left().wait_recv()

    for m in range(2):
        packed = jnp.where(
            iota((own_rows, EDGE), 1) < EDGE // 2, halo[1, m].astype(F32), halo[0, m].astype(F32)
        )
        edge[m] = packed.astype(BF16)
    for e, w in order:
        edge_copy(e, w, p).start()
    slab[pl.ds(p * own_rows, own_rows), 0:EDGE] = edge[k]

    for w in range(1, 4):
        cell_near(w, True).wait_recv()
    for w in range(1, ty):
        cell_y(w, False).start()
    cell_two[y] = cell_one[:, :, y]
    bands(1)
    bands(2)
    for w in range(1, ty):
        cell_y(w, True).wait_recv()
    for w in range(1, tx):
        cell_x(w, False).start()
    cell_in[x] = cell_two[:, :, x]
    bands(3)
    for b in range(blocks):
        lanes = pl.ds(b * 128, 128)
        for m in range(2):
            start_xy[m, b : b + 1, :] = positions[m : m + 1, lanes]
    for w in range(1, tx):
        cell_x(w, True).wait_recv()
    offsets[...] = cell_in[...] >> 7
    to_scalars = pltpu.make_async_copy(offsets, offset_of, load_sem.at[len(loads)])
    to_scalars.start()

    for e, w in order:
        kappa_copy(e, w, column_mate(e, w)).wait_recv()
    for e, w in order:
        edge_copy(e, w, column_mate(e, w)).wait_recv()
    slab[:, EDGE + cols :] = slab[:, 0:EDGE]

    for j in range(cols // EDGE):
        window = slab[:, j * EDGE : j * EDGE + WIDE]
        passed = dot_t(window, col_high[...]) + dot_t(window, col_low[...])
        for c in range(4):
            lanes = slice(j * EDGE, (j + 1) * EDGE)
            pass_high[c, :, lanes], pass_low[c, :, lanes] = split(passed[:, c * EDGE : (c + 1) * EDGE])
    strips = cols // 128
    flat_rows = rows_of.reshape(rows * cols // 16, 128)
    for c in range(CHANNELS):
        if c < 4:
            field = (
                dot(row_high[c], pass_high[c]) + dot(row_low[c], pass_high[c]) + dot(row_high[c], pass_low[c])
            ).astype(BF16)
        else:
            field = slab[:, EDGE : EDGE + cols]
        table[c * rows : (c + 1) * rows, :] = field
        exact = field.astype(F32)
        for j in range(strips):
            flat_rows[pl.ds(j * 8 + c, rows, stride=8 * strips), :] = exact[:, j * 128 : (j + 1) * 128]
    to_scalars.wait()

    lane = iota((8, 128), 1)
    sublane = iota((8, 128), 0)

    def place(u):
        kk, t = peer(u)
        return t // (2 * ty), mod(t // 2, ty), mod(t, 2) * 2 + kk

    def by_matmul(u):
        ids = cell_in[place(u)]
        hot = (iota((cols, 256), 0) == (ids & (cols - 1))).astype(F32).astype(BF16)
        picked = dot(table[...], hot)
        mine = iota((rows, 256), 0) == (ids >> 9)
        values = [
            jnp.sum(jnp.where(mine, picked[c * rows : (c + 1) * rows], 0.0), axis=0, keepdims=True)
            for c in range(CHANNELS)
        ]
        pad = [jnp.zeros((3, 128), F32)]
        return jnp.concatenate([v[:, :128] for v in values] + pad + [v[:, 128:] for v in values] + pad, axis=0)

    def by_rows(u):
        px, py, pq = place(u)
        slots = []
        for slot in range(2):
            low = cell_in[px, py, pq, :, slot * 128 : (slot + 1) * 128] & 127
            low = jnp.broadcast_to(low, (8, 128))
            sums = [jnp.zeros((8, 128), F32) for _ in range(4)]
            for n in range(128):
                picked = jnp.take_along_axis(rows_of[offset_of[px, py, pq, 0, slot * 128 + n]], low, axis=1)
                sums[n % 4] = jnp.where(lane == n, picked, sums[n % 4])
            total = (sums[0] + sums[1]) + (sums[2] + sums[3])
            slots.append(jnp.where(sublane < CHANNELS, total, 0.0))
        return jnp.concatenate(slots, axis=0)

    def found_copy(u, arrival):
        kk, t = peer(u)
        slot = (kk, t) if arrival else (k, r)
        return remote(
            found.at[u], samples.at[slot], found_send.at[u], found_recv.at[slot], base + kk, t
        )

    @pl.loop(0, peers // GROUP)
    def _(g):
        for i in range(GROUP):
            u = g * GROUP + i
            found[u] = (by_matmul if i < GROUP // 2 else by_rows)(u).astype(BF16)

        @pl.when(g > 0)
        def _():
            found_copy(g * GROUP, False).start()

        for i in range(1, GROUP):
            found_copy(g * GROUP + i, False).start()

    samples[k, r] = found[0]

    @pl.loop(1, peers)
    def _(u):
        found_copy(u, True).wait_recv()

    initial = (start_xy[0], start_xy[1], 1.0, 0.0, 0.0, 1.0)
    state = (start_xy[0], start_xy[1]) + tuple(
        jnp.full((blocks, 128), v, F32) for v in initial[2:]
    )
    for m in range(2):
        target = jnp.concatenate([target_cols[m] * 8 + c for c in range(CHANNELS)], axis=0)
        wanted = (iota((CHANNELS * blocks, tiles * 16), 1) == target).astype(F32).astype(BF16)
        got = dot(wanted, samples[m].reshape(tiles * 16, 128))
        state = advance(
            state, [got[c * blocks : (c + 1) * blocks] for c in range(CHANNELS)], LENS_WEIGHTS[m]
        )
    for v in range(6):
        value = jnp.where(traced_col, state[v], initial[v])
        ref, row = (final, v) if v < 2 else (jacobian, v - 2)
        for b in range(blocks):
            ref[row : row + 1, b * 128 : (b + 1) * 128] = value[b : b + 1]

    @pl.when(r < tiles - 1)
    def _():
        to_right().wait_send()

    @pl.when(r > 0)
    def _():
        to_left().wait_send()

    for e, w in order:
        kappa_copy(e, w, p).wait_send()
        edge_copy(e, w, p).wait_send()
    for w in range(1, 4):
        cell_near(w, False).wait_send()
    for w in range(1, ty):
        cell_y(w, False).wait_send()
    for w in range(1, tx):
        cell_x(w, False).wait_send()

    @pl.loop(1, peers)
    def _(u):
        found_copy(u, False).wait_send()


def local(planes, tiles, kappa, row_kernel, col_kernel, positions, cells, owners, counts):
    own_rows, cols = kappa.shape[1:]
    rows = planes * own_rows
    blocks = owners.shape[1]
    rays = positions.shape[1]
    peers = 2 * tiles
    grid = (tiles // 8, 4)
    in_vmem = pl.BlockSpec(memory_space=pltpu.VMEM)
    in_hbm = pl.BlockSpec(memory_space=pltpu.HBM)
    dma = pltpu.SemaphoreType.DMA
    vmem = pltpu.VMEM
    ints = jnp.int32
    return pl.pallas_call(
        functools.partial(kernel, planes, grid),
        out_shape=(
            jax.ShapeDtypeStruct((2, rays), F32),
            jax.ShapeDtypeStruct((4, rays), F32),
        ),
        in_specs=[in_hbm] * 6 + [pl.BlockSpec(memory_space=pltpu.SMEM)],
        out_specs=(in_vmem, in_vmem),
        scratch_shapes=[
            vmem(row_kernel.shape, F32),
            vmem(col_kernel.shape, F32),
            vmem(positions.shape, F32),
            vmem(cells.shape, ints),
            vmem((2, 1, blocks), ints),
            vmem((rows, cols + 2 * EDGE), BF16),
            vmem((2, 2, own_rows, EDGE), BF16),
            vmem((2, own_rows, EDGE), BF16),
            vmem((8, WIDE), F32),
            vmem((4 * EDGE, WIDE), BF16),
            vmem((4 * EDGE, WIDE), BF16),
            vmem((4, rows, rows), BF16),
            vmem((4, rows, rows), BF16),
            vmem((4, rows, cols), BF16),
            vmem((4, rows, cols), BF16),
            vmem((CHANNELS * rows, cols), BF16),
            vmem((rows * cols // 128, 8, 128), F32),
            vmem((2, blocks, 128), F32),
            vmem((2, blocks, 128), ints),
            vmem((4,) + grid + (1, 256), ints),
            vmem((4,) + grid + (1, 256), ints),
            vmem((grid[1], 4, grid[0], 1, 256), ints),
            vmem(grid + (4, 1, 256), ints),
            vmem(grid + (4, 1, 256), ints),
            pltpu.SMEM(grid + (4, 1, 256), ints),
            vmem((peers, 16, 128), BF16),
            vmem((2, tiles, 16, 128), BF16),
            dma((7,)),
            dma((2,)),
            dma((2,)),
            dma((planes // 2, 2)),
            dma((planes,)),
            dma((planes // 2, 2)),
            dma((planes,)),
            dma((3, 4)),
            dma((3, 4)),
            dma((peers,)),
            dma((2, tiles)),
        ],
        compiler_params=pltpu.CompilerParams(
            collective_id=0, has_side_effects=True, vmem_limit_bytes=60 * 2**20
        ),
    )(kappa, row_kernel, col_kernel, positions, cells, owners.reshape(2, 1, blocks), counts)


def solution(mesh):
    return jax.shard_map(
        functools.partial(local, mesh.shape["plane"], mesh.shape["ray"]),
        mesh=mesh,
        in_specs=(
            P(None, "plane", "ray"),
            P(),
            P(),
            P(None, ("plane", "ray")),
            P(None, ("plane", "ray")),
            P(None, ("plane", "ray"), None),
            P(("plane", "ray")),
        ),
        out_specs=(P(None, ("plane", "ray")), P(None, ("plane", "ray"))),
        check_vma=False,
    )
```

```python
import functools
import jax
import jax.numpy as jnp
from jax import lax
from jax.experimental import pallas as pl
from jax.experimental.pallas import tpu as pltpu
from jax.sharding import PartitionSpec as P

MESH = pl.DeviceIdType.MESH
LENS_WEIGHTS = (0.6, 0.4)
CHANNELS = 5
EDGE = 128
WIDE = 384
GROUP = 8
F32 = jnp.float32
BF16 = jnp.bfloat16


def iota(shape, dim):
    return lax.broadcasted_iota(jnp.int32, shape, dim)


def mod(a, b):
    return a & (b - 1)


def split(x):
    high = x.astype(BF16)
    return high, (x - high.astype(F32)).astype(BF16)


def dot(a, b):
    return jnp.dot(a, b, preferred_element_type=F32)


def dot_t(a, b):
    return lax.dot_general(a, b, (((1,), (1,)), ((), ())), preferred_element_type=F32)


def advance(ray_state, samples, plane_weight):
    pos_x, pos_y, jac_xx, jac_xy, jac_yx, jac_yy = ray_state
    deflect_x, deflect_y, shear_one, shear_two, converge = samples
    mat_xx = converge + shear_one
    mat_yy = converge - shear_one
    return (
        pos_x - plane_weight * deflect_x,
        pos_y - plane_weight * deflect_y,
        jac_xx - plane_weight * (mat_xx * jac_xx + shear_two * jac_yx),
        jac_xy - plane_weight * (mat_xx * jac_xy + shear_two * jac_yy),
        jac_yx - plane_weight * (shear_two * jac_xx + mat_yy * jac_yx),
        jac_yy - plane_weight * (shear_two * jac_xy + mat_yy * jac_yy),
    )


def kernel(
    planes, tiles,
    kappa_hbm, row_kernel_hbm, col_kernel_hbm, positions_hbm, cells_hbm, owners_hbm, counts,
    final, jacobian,
    row_kernel, col_kernel, positions, cells, owners,
    slab, halo, edge, taps, col_high, col_low, row_high, row_low, pass_high, pass_low, table, rows_of,
    start_xy, cell_rows, cell_out, cell_one, cell_mid, cell_in, offsets, offset_of, found, samples,
    load_sem, halo_send, halo_recv, kappa_send, kappa_recv, edge_send, edge_recv,
    near_send, near_recv, cell_send, cell_recv, found_send, found_recv,
):
    groups = tiles // 2
    p, r = lax.axis_index("plane"), lax.axis_index("ray")
    k = mod(p, 2)
    base = p - k
    home, zl = r >> 1, mod(r, 2)
    near = zl * 2 + k
    own_rows, cols = kappa_hbm.shape[1:]
    rows = planes * own_rows
    blocks = owners.shape[2]
    peers = 2 * tiles
    margin = (row_kernel.shape[1] - 1) // 2

    def peer(u):
        return mod(k + u, 2), mod(r + (u >> 1), tiles)

    def near_mate(w):
        q = mod(near + w, 4)
        return q, base + mod(q, 2), r - zl + (q >> 1)

    def group_mate(w):
        other = mod(home + w, groups)
        return other, r + 2 * (other - home)

    def column_mate(e, w):
        return mod(base + 2 * e, planes) + mod(k + w, 2)

    half = planes // 2
    order = [
        (e, w) for e in sorted(range(half), key=lambda e: -min(e, half - e)) for w in (1, 0) if (e, w) != (0, 0)
    ]
    far = [(e, w) for e, w in order if e]

    barrier = pltpu.get_barrier_semaphore()

    def greet(dp, dr):
        pl.semaphore_signal(barrier, inc=1, device_id=(dp, dr), device_id_type=MESH)

    @pl.when(r > 0)
    def _():
        greet(p, r - 1)

    @pl.when(r < tiles - 1)
    def _():
        greet(p, r + 1)

    for w in range(1, 4):
        greet(*near_mate(w)[1:])
    for e, w in far:
        greet(column_mate(e, w), r)
    for w in range(1, groups):
        greet(p, group_mate(w)[1])

    loads = [
        pltpu.make_async_copy(src, dst, load_sem.at[i])
        for i, (src, dst) in enumerate([
            (owners_hbm, owners),
            (cells_hbm, cells),
            (row_kernel_hbm, row_kernel),
            (col_kernel_hbm, col_kernel),
            (positions_hbm, positions),
            (kappa_hbm.at[k], slab.at[pl.ds(p * own_rows, own_rows), pl.ds(EDGE, cols)]),
        ])
    ]
    for load in loads:
        load.start()
    for load in loads[:2]:
        load.wait()

    for b in range(blocks):
        lanes = pl.ds(b * 128, 128)
        for m in range(2):
            cell_rows[m, b : b + 1, :] = cells[m : m + 1, lanes]
    left_id = iota((blocks, blocks), 0)
    right_id = iota((blocks, blocks), 1)
    traced_row = iota((1, blocks), 1) < counts[0]
    traced_col = iota((blocks, 1), 0) < counts[0]
    target_cols = []
    for m in range(2):
        owner_row = owners[m]
        owner_col = jnp.sum(
            jnp.where(left_id == right_id, jnp.broadcast_to(owner_row, (blocks, blocks)), 0),
            axis=1, keepdims=True,
        )
        same = owner_col == owner_row
        slot_row = jnp.sum((same & (left_id < right_id)).astype(jnp.int32), axis=0, keepdims=True)
        slot_col = jnp.sum((same & (right_id < left_id)).astype(jnp.int32), axis=1, keepdims=True)
        dest_row = jnp.where(
            traced_row, (owner_row & 1) * tiles + (owner_row >> 1) * 2 + slot_row, -1
        )
        target_cols.append(jnp.where(traced_col, owner_col * 2 + slot_col, -1))
        choose = (iota((peers, blocks), 0) == dest_row).astype(jnp.int32)
        ids = cell_rows[m]
        out = sum(choose[:, b : b + 1] * ids[b : b + 1] for b in range(blocks))
        for z in range(2):
            cell_out[z * 2 + m] = out[z * tiles : (z + 1) * tiles]

    sides = jnp.minimum(r, 1) + jnp.minimum(tiles - 1 - r, 1)
    pl.semaphore_wait(barrier, 3 + len(far) + groups - 1 + sides)

    def remote(src, dst, send_sem, recv_sem, dp, dr):
        return pltpu.make_async_remote_copy(
            src_ref=src, dst_ref=dst, send_sem=send_sem, recv_sem=recv_sem,
            device_id=(dp, dr), device_id_type=MESH,
        )

    def to_right():
        return remote(
            kappa_hbm.at[:, :, pl.ds(cols - EDGE, EDGE)], halo.at[0], halo_send.at[0], halo_recv.at[0], p, r + 1
        )

    def to_left():
        return remote(
            kappa_hbm.at[:, :, pl.ds(0, EDGE)], halo.at[1], halo_send.at[1], halo_recv.at[1], p, r - 1
        )

    def own_part(q, lanes):
        return slab.at[pl.ds(q * own_rows, own_rows), lanes]

    def kappa_copy(e, w, sender):
        return remote(
            kappa_hbm.at[mod(k + w, 2)], own_part(sender, pl.ds(EDGE, cols)),
            kappa_send.at[e, w], kappa_recv.at[sender], column_mate(e, w), r,
        )

    def edge_copy(e, w, sender):
        return remote(
            edge.at[mod(k + w, 2)], own_part(sender, pl.ds(0, EDGE)),
            edge_send.at[e, w], edge_recv.at[sender], column_mate(e, w), r,
        )

    def cell_near(w, arrival):
        q, dp, dr = near_mate(w)
        slot = q if arrival else near
        return remote(cell_out.at[q], cell_one.at[slot], near_send.at[w], near_recv.at[slot], dp, dr)

    def cell_far(w):
        other, dr = group_mate(w)
        return remote(
            cell_mid.at[other], cell_in.at[home], cell_send.at[0], cell_recv.at[0], p, dr
        )

    def all_cells():
        most = pl.ds(0, groups - 1)
        return remote(cell_mid.at[most], cell_in.at[most], cell_send.at[0], cell_recv.at[0], p, r)

    @pl.when(r < tiles - 1)
    def _():
        to_right().start()

    @pl.when(r > 0)
    def _():
        to_left().start()

    for w in range(1, 4):
        cell_near(w, False).start()
    for e, w in order:
        kappa_copy(e, w, p).start()
    cell_one[near] = cell_out[near]

    @pl.when(r == 0)
    def _():
        halo[0] = jnp.zeros(halo.shape[1:], BF16)

    @pl.when(r == tiles - 1)
    def _():
        halo[1] = jnp.zeros(halo.shape[1:], BF16)

    for load in loads[2:]:
        load.wait()

    taps[...] = jnp.zeros_like(taps)
    taps[0:4, 0 : row_kernel.shape[1]] = row_kernel[...]
    taps[4:8, 0 : row_kernel.shape[1]] = col_kernel[...]

    def bands(c):
        across = jnp.broadcast_to(taps[4 + c : 5 + c, :], (EDGE, WIDE))
        band = pltpu.roll(across, EDGE - margin, 1, stride=1, stride_axis=0)
        col_high[c * EDGE : (c + 1) * EDGE, :], col_low[c * EDGE : (c + 1) * EDGE, :] = split(band)
        down = jnp.broadcast_to(taps[c : c + 1, :], (rows, WIDE))
        band = pltpu.roll(down, WIDE - margin, 1, stride=1, stride_axis=0)[:, :rows]
        row_high[c], row_low[c] = split(band)

    bands(0)

    @pl.when(r > 0)
    def _():
        to_right().wait_recv()

    @pl.when(r < tiles - 1)
    def _():
        to_left().wait_recv()

    for m in range(2):
        packed = jnp.where(
            iota((own_rows, EDGE), 1) < EDGE // 2, halo[1, m].astype(F32), halo[0, m].astype(F32)
        )
        edge[m] = packed.astype(BF16)
    for e, w in order:
        edge_copy(e, w, p).start()
    slab[pl.ds(p * own_rows, own_rows), 0:EDGE] = edge[k]

    for w in range(1, 4):
        cell_near(w, True).wait_recv()
    for q in range(4):
        for g in range(groups):
            cell_mid[g, 2 * q : 2 * q + 2, :] = cell_one[q, 2 * g : 2 * g + 2, :]
    for w in range(1, groups):
        cell_far(w).start()
    cell_in[home] = cell_mid[home]
    bands(1)
    bands(2)
    bands(3)
    for b in range(blocks):
        lanes = pl.ds(b * 128, 128)
        for m in range(2):
            start_xy[m, b : b + 1, :] = positions[m : m + 1, lanes]
    all_cells().wait_recv()
    offsets[...] = cell_in[...] >> 7
    to_scalars = pltpu.make_async_copy(offsets, offset_of, load_sem.at[len(loads)])
    to_scalars.start()

    for e, w in order:
        kappa_copy(e, w, column_mate(e, w)).wait_recv()
    for e, w in order:
        edge_copy(e, w, column_mate(e, w)).wait_recv()
    slab[:, EDGE + cols :] = slab[:, 0:EDGE]

    for j in range(cols // EDGE):
        window = slab[:, j * EDGE : j * EDGE + WIDE]
        passed = dot_t(window, col_high[...]) + dot_t(window, col_low[...])
        for c in range(4):
            lanes = slice(j * EDGE, (j + 1) * EDGE)
            pass_high[c, :, lanes], pass_low[c, :, lanes] = split(passed[:, c * EDGE : (c + 1) * EDGE])
    strips = cols // 128
    flat_rows = rows_of.reshape(rows * cols // 16, 128)
    for c in range(CHANNELS):
        if c < 4:
            field = (
                dot(row_high[c], pass_high[c]) + dot(row_low[c], pass_high[c]) + dot(row_high[c], pass_low[c])
            ).astype(BF16)
        else:
            field = slab[:, EDGE : EDGE + cols]
        table[c * rows : (c + 1) * rows, :] = field
        exact = field.astype(F32)
        for j in range(strips):
            flat_rows[pl.ds(j * 8 + c, rows, stride=8 * strips), :] = exact[:, j * 128 : (j + 1) * 128]
    to_scalars.wait()

    lane = iota((8, 128), 1)
    sublane = iota((8, 128), 0)

    def place(u, slot):
        kk, t = peer(u)
        return t >> 1, (mod(t, 2) * 2 + kk) * 2 + slot

    def ids_of(u, slot):
        group, row = place(u, slot)
        return cell_in[group, pl.ds(row, 1), :]

    def by_matmul(u):
        ids = jnp.concatenate([ids_of(u, 0), ids_of(u, 1)], axis=1)
        hot = (iota((cols, 256), 0) == (ids & (cols - 1))).astype(F32).astype(BF16)
        picked = dot(table[...], hot)
        mine = iota((rows, 256), 0) == (ids >> 9)
        values = [
            jnp.sum(jnp.where(mine, picked[c * rows : (c + 1) * rows], 0.0), axis=0, keepdims=True)
            for c in range(CHANNELS)
        ]
        pad = [jnp.zeros((3, 128), F32)]
        return jnp.concatenate([v[:, :128] for v in values] + pad + [v[:, 128:] for v in values] + pad, axis=0)

    def by_rows(u):
        slots = []
        for slot in range(2):
            group, row = place(u, slot)
            low = jnp.broadcast_to(ids_of(u, slot) & 127, (8, 128))
            sums = [jnp.zeros((8, 128), F32) for _ in range(4)]
            for n in range(128):
                picked = jnp.take_along_axis(rows_of[offset_of[group, row, n]], low, axis=1)
                sums[n % 4] = jnp.where(lane == n, picked, sums[n % 4])
            total = (sums[0] + sums[1]) + (sums[2] + sums[3])
            slots.append(jnp.where(sublane < CHANNELS, total, 0.0))
        return jnp.concatenate(slots, axis=0)

    def found_copy(u):
        kk, t = peer(u)
        return remote(
            found.at[u], samples.at[k * tiles + r], found_send.at[0], found_recv.at[0], base + kk, t
        )

    def all_found():
        most = pl.ds(0, peers - 1)
        return remote(found.at[most], samples.at[most], found_send.at[0], found_recv.at[0], p, r)

    @pl.loop(0, peers // GROUP)
    def _(g):
        for i in range(GROUP):
            u = g * GROUP + i
            found[u] = (by_matmul if i < GROUP // 2 else by_rows)(u).astype(BF16)

        @pl.when(g > 0)
        def _():
            found_copy(g * GROUP).start()

        for i in range(1, GROUP):
            found_copy(g * GROUP + i).start()

    samples[k * tiles + r] = found[0]
    all_found().wait_recv()

    initial = (start_xy[0], start_xy[1], 1.0, 0.0, 0.0, 1.0)
    state = (start_xy[0], start_xy[1]) + tuple(
        jnp.full((blocks, 128), v, F32) for v in initial[2:]
    )
    for m in range(2):
        target = jnp.concatenate([target_cols[m] * 8 + c for c in range(CHANNELS)], axis=0)
        wanted = (iota((CHANNELS * blocks, tiles * 16), 1) == target).astype(F32).astype(BF16)
        got = dot(wanted, samples[m * tiles : (m + 1) * tiles].reshape(tiles * 16, 128))
        state = advance(
            state, [got[c * blocks : (c + 1) * blocks] for c in range(CHANNELS)], LENS_WEIGHTS[m]
        )
    for v in range(6):
        value = jnp.where(traced_col, state[v], initial[v])
        ref, row = (final, v) if v < 2 else (jacobian, v - 2)
        for b in range(blocks):
            ref[row : row + 1, b * 128 : (b + 1) * 128] = value[b : b + 1]

    @pl.when(r < tiles - 1)
    def _():
        to_right().wait_send()

    @pl.when(r > 0)
    def _():
        to_left().wait_send()

    for e, w in order:
        kappa_copy(e, w, p).wait_send()
        edge_copy(e, w, p).wait_send()
    for w in range(1, 4):
        cell_near(w, False).wait_send()
    all_cells().wait_send()
    all_found().wait_send()


def local(planes, tiles, kappa, row_kernel, col_kernel, positions, cells, owners, counts):
    own_rows, cols = kappa.shape[1:]
    rows = planes * own_rows
    blocks = owners.shape[1]
    rays = positions.shape[1]
    peers = 2 * tiles
    in_vmem = pl.BlockSpec(memory_space=pltpu.VMEM)
    in_hbm = pl.BlockSpec(memory_space=pltpu.HBM)
    dma = pltpu.SemaphoreType.DMA
    vmem = pltpu.VMEM
    ints = jnp.int32
    return pl.pallas_call(
        functools.partial(kernel, planes, tiles),
        out_shape=(
            jax.ShapeDtypeStruct((2, rays), F32),
            jax.ShapeDtypeStruct((4, rays), F32),
        ),
        in_specs=[in_hbm] * 6 + [pl.BlockSpec(memory_space=pltpu.SMEM)],
        out_specs=(in_vmem, in_vmem),
        scratch_shapes=[
            vmem(row_kernel.shape, F32),
            vmem(col_kernel.shape, F32),
            vmem(positions.shape, F32),
            vmem(cells.shape, ints),
            vmem((2, 1, blocks), ints),
            vmem((rows, cols + 2 * EDGE), BF16),
            vmem((2, 2, own_rows, EDGE), BF16),
            vmem((2, own_rows, EDGE), BF16),
            vmem((8, WIDE), F32),
            vmem((4 * EDGE, WIDE), BF16),
            vmem((4 * EDGE, WIDE), BF16),
            vmem((4, rows, rows), BF16),
            vmem((4, rows, rows), BF16),
            vmem((4, rows, cols), BF16),
            vmem((4, rows, cols), BF16),
            vmem((CHANNELS * rows, cols), BF16),
            vmem((rows * cols // 128, 8, 128), F32),
            vmem((2, blocks, 128), F32),
            vmem((2, blocks, 128), ints),
            vmem((4, tiles, 128), ints),
            vmem((4, tiles, 128), ints),
            vmem((tiles // 2, 8, 128), ints),
            vmem((tiles // 2, 8, 128), ints),
            vmem((tiles // 2, 8, 128), ints),
            pltpu.SMEM((tiles // 2, 8, 128), ints),
            vmem((peers, 16, 128), BF16),
            vmem((peers, 16, 128), BF16),
            dma((7,)),
            dma((2,)),
            dma((2,)),
            dma((planes // 2, 2)),
            dma((planes,)),
            dma((planes // 2, 2)),
            dma((planes,)),
            dma((4,)),
            dma((4,)),
            dma((1,)),
            dma((1,)),
            dma((1,)),
            dma((1,)),
        ],
        compiler_params=pltpu.CompilerParams(
            collective_id=0, has_side_effects=True, vmem_limit_bytes=60 * 2**20
        ),
    )(kappa, row_kernel, col_kernel, positions, cells, owners.reshape(2, 1, blocks), counts)


def solution(mesh):
    return jax.shard_map(
        functools.partial(local, mesh.shape["plane"], mesh.shape["ray"]),
        mesh=mesh,
        in_specs=(
            P(None, "plane", "ray"),
            P(),
            P(),
            P(None, ("plane", "ray")),
            P(None, ("plane", "ray")),
            P(None, ("plane", "ray"), None),
            P(("plane", "ray")),
        ),
        out_specs=(P(None, ("plane", "ray")), P(None, ("plane", "ray"))),
        check_vma=False,
    )
```

```python
import functools
import jax
import jax.numpy as jnp
from jax import lax
from jax.experimental import pallas as pl
from jax.experimental.pallas import tpu as pltpu
from jax.sharding import PartitionSpec as P

MESH = pl.DeviceIdType.MESH
LENS_WEIGHTS = (0.6, 0.4)
CHANNELS = 5
EDGE = 128
WIDE = 384
GROUP = 8
F32 = jnp.float32
BF16 = jnp.bfloat16


def iota(shape, dim):
    return lax.broadcasted_iota(jnp.int32, shape, dim)


def mod(a, b):
    return a & (b - 1)


def split(x):
    high = x.astype(BF16)
    return high, (x - high.astype(F32)).astype(BF16)


def dot(a, b):
    return jnp.dot(a, b, preferred_element_type=F32)


def dot_t(a, b):
    return lax.dot_general(a, b, (((1,), (1,)), ((), ())), preferred_element_type=F32)


def advance(ray_state, samples, plane_weight):
    pos_x, pos_y, jac_xx, jac_xy, jac_yx, jac_yy = ray_state
    deflect_x, deflect_y, shear_one, shear_two, converge = samples
    mat_xx = converge + shear_one
    mat_yy = converge - shear_one
    return (
        pos_x - plane_weight * deflect_x,
        pos_y - plane_weight * deflect_y,
        jac_xx - plane_weight * (mat_xx * jac_xx + shear_two * jac_yx),
        jac_xy - plane_weight * (mat_xx * jac_xy + shear_two * jac_yy),
        jac_yx - plane_weight * (shear_two * jac_xx + mat_yy * jac_yx),
        jac_yy - plane_weight * (shear_two * jac_xy + mat_yy * jac_yy),
    )


def kernel(
    planes, tiles,
    kappa_hbm, row_kernel_hbm, col_kernel_hbm, positions_hbm, cells_hbm, owners_hbm, counts_hbm,
    final, jacobian,
    row_kernel, col_kernel, positions, cells, owners, counts,
    slab, halo, edge, taps, col_high, col_low, row_high, row_low, pass_high, pass_low, table, rows_of,
    start_xy, cell_rows, cell_out, cell_one, cell_mid, cell_in, offsets, offset_of, found, samples,
    load_sem, halo_send, halo_recv, kappa_send, kappa_recv, edge_send, edge_recv,
    near_send, near_recv, cell_send, cell_recv, found_send, found_recv,
):
    groups = tiles // 2
    p, r = lax.axis_index("plane"), lax.axis_index("ray")
    k = mod(p, 2)
    base = p - k
    home, zl = r >> 1, mod(r, 2)
    near = zl * 2 + k
    own_rows, cols = kappa_hbm.shape[1:]
    rows = planes * own_rows
    blocks = owners.shape[2]
    peers = 2 * tiles
    margin = (row_kernel.shape[1] - 1) // 2

    def peer(u):
        return mod(k + u, 2), mod(r + (u >> 1), tiles)

    def near_mate(w):
        q = mod(near + w, 4)
        return q, base + mod(q, 2), r - zl + (q >> 1)

    def group_mate(w):
        other = mod(home + w, groups)
        return other, r + 2 * (other - home)

    def column_mate(e, w):
        return mod(base + 2 * e, planes) + mod(k + w, 2)

    half = planes // 2
    order = [
        (e, w) for e in sorted(range(half), key=lambda e: -min(e, half - e)) for w in (1, 0) if (e, w) != (0, 0)
    ]
    far = [(e, w) for e, w in order if e]

    loads = [
        pltpu.make_async_copy(src, dst, load_sem.at[i])
        for i, (src, dst) in enumerate([
            (owners_hbm, owners),
            (cells_hbm, cells),
            (counts_hbm, counts),
            (row_kernel_hbm, row_kernel),
            (col_kernel_hbm, col_kernel),
            (positions_hbm, positions),
            (kappa_hbm.at[k], slab.at[pl.ds(p * own_rows, own_rows), pl.ds(EDGE, cols)]),
        ])
    ]
    for load in loads[:3]:
        load.start()

    barrier = pltpu.get_barrier_semaphore()

    def greet(dp, dr):
        pl.semaphore_signal(barrier, inc=1, device_id=(dp, dr), device_id_type=MESH)

    @pl.when(r > 0)
    def _():
        greet(p, r - 1)

    @pl.when(r < tiles - 1)
    def _():
        greet(p, r + 1)

    for w in range(1, 4):
        greet(*near_mate(w)[1:])
    for e, w in far:
        greet(column_mate(e, w), r)
    for w in range(1, groups):
        greet(p, group_mate(w)[1])

    for load in loads[:3]:
        load.wait()

    for b in range(blocks):
        lanes = pl.ds(b * 128, 128)
        for m in range(2):
            cell_rows[m, b : b + 1, :] = cells[m : m + 1, lanes]
    left_id = iota((blocks, blocks), 0)
    right_id = iota((blocks, blocks), 1)
    traced_row = iota((1, blocks), 1) < counts[0]
    traced_col = iota((blocks, 1), 0) < counts[0]
    target_cols = []
    for m in range(2):
        owner_row = owners[m]
        owner_col = jnp.sum(
            jnp.where(left_id == right_id, jnp.broadcast_to(owner_row, (blocks, blocks)), 0),
            axis=1, keepdims=True,
        )
        same = owner_col == owner_row
        slot_row = jnp.sum((same & (left_id < right_id)).astype(jnp.int32), axis=0, keepdims=True)
        slot_col = jnp.sum((same & (right_id < left_id)).astype(jnp.int32), axis=1, keepdims=True)
        dest_row = jnp.where(
            traced_row, (owner_row & 1) * tiles + (owner_row >> 1) * 2 + slot_row, -1
        )
        target_cols.append(jnp.where(traced_col, owner_col * 2 + slot_col, -1))
        choose = (iota((peers, blocks), 0) == dest_row).astype(jnp.int32)
        ids = cell_rows[m]
        out = sum(choose[:, b : b + 1] * ids[b : b + 1] for b in range(blocks))
        for z in range(2):
            cell_out[z * 2 + m] = out[z * tiles : (z + 1) * tiles]

    sides = jnp.minimum(r, 1) + jnp.minimum(tiles - 1 - r, 1)
    pl.semaphore_wait(barrier, 3 + len(far) + groups - 1 + sides)

    def remote(src, dst, send_sem, recv_sem, dp, dr):
        return pltpu.make_async_remote_copy(
            src_ref=src, dst_ref=dst, send_sem=send_sem, recv_sem=recv_sem,
            device_id=(dp, dr), device_id_type=MESH,
        )

    def to_right():
        return remote(
            kappa_hbm.at[:, :, pl.ds(cols - EDGE, EDGE)], halo.at[0], halo_send.at[0], halo_recv.at[0], p, r + 1
        )

    def to_left():
        return remote(
            kappa_hbm.at[:, :, pl.ds(0, EDGE)], halo.at[1], halo_send.at[1], halo_recv.at[1], p, r - 1
        )

    def own_part(q, lanes):
        return slab.at[pl.ds(q * own_rows, own_rows), lanes]

    def kappa_copy(e, w, sender):
        return remote(
            kappa_hbm.at[mod(k + w, 2)], own_part(sender, pl.ds(EDGE, cols)),
            kappa_send.at[e, w], kappa_recv.at[sender], column_mate(e, w), r,
        )

    def edge_copy(e, w, sender):
        return remote(
            edge.at[mod(k + w, 2)], own_part(sender, pl.ds(0, EDGE)),
            edge_send.at[e, w], edge_recv.at[sender], column_mate(e, w), r,
        )

    def cell_near(w, arrival):
        q, dp, dr = near_mate(w)
        slot = q if arrival else near
        return remote(cell_out.at[q], cell_one.at[slot], near_send.at[w], near_recv.at[slot], dp, dr)

    def cell_far(w):
        other, dr = group_mate(w)
        return remote(
            cell_mid.at[other], cell_in.at[home], cell_send.at[0], cell_recv.at[0], p, dr
        )

    def all_cells():
        most = pl.ds(0, groups - 1)
        return remote(cell_mid.at[most], cell_in.at[most], cell_send.at[0], cell_recv.at[0], p, r)

    @pl.when(r < tiles - 1)
    def _():
        to_right().start()

    @pl.when(r > 0)
    def _():
        to_left().start()

    for w in range(1, 4):
        cell_near(w, False).start()
    for e, w in order:
        kappa_copy(e, w, p).start()
    for load in loads[3:]:
        load.start()
    cell_one[near] = cell_out[near]

    @pl.when(r == 0)
    def _():
        halo[0] = jnp.zeros(halo.shape[1:], BF16)

    @pl.when(r == tiles - 1)
    def _():
        halo[1] = jnp.zeros(halo.shape[1:], BF16)

    for load in loads[3:]:
        load.wait()

    taps[...] = jnp.zeros_like(taps)
    taps[0:4, 0 : row_kernel.shape[1]] = row_kernel[...]
    taps[4:8, 0 : row_kernel.shape[1]] = col_kernel[...]

    def bands(c):
        across = jnp.broadcast_to(taps[4 + c : 5 + c, :], (EDGE, WIDE))
        band = pltpu.roll(across, EDGE - margin, 1, stride=1, stride_axis=0)
        col_high[c * EDGE : (c + 1) * EDGE, :], col_low[c * EDGE : (c + 1) * EDGE, :] = split(band)
        down = jnp.broadcast_to(taps[c : c + 1, :], (rows, WIDE))
        band = pltpu.roll(down, WIDE - margin, 1, stride=1, stride_axis=0)[:, :rows]
        row_high[c], row_low[c] = split(band)

    bands(0)

    @pl.when(r > 0)
    def _():
        to_right().wait_recv()

    @pl.when(r < tiles - 1)
    def _():
        to_left().wait_recv()

    for m in range(2):
        packed = jnp.where(
            iota((own_rows, EDGE), 1) < EDGE // 2, halo[1, m].astype(F32), halo[0, m].astype(F32)
        )
        edge[m] = packed.astype(BF16)
    for e, w in order:
        edge_copy(e, w, p).start()
    slab[pl.ds(p * own_rows, own_rows), 0:EDGE] = edge[k]

    for w in range(1, 4):
        cell_near(w, True).wait_recv()
    for q in range(4):
        for g in range(groups):
            cell_mid[g, 2 * q : 2 * q + 2, :] = cell_one[q, 2 * g : 2 * g + 2, :]
    for w in range(1, groups):
        cell_far(w).start()
    cell_in[home] = cell_mid[home]
    bands(1)
    bands(2)
    bands(3)
    for b in range(blocks):
        lanes = pl.ds(b * 128, 128)
        for m in range(2):
            start_xy[m, b : b + 1, :] = positions[m : m + 1, lanes]
    all_cells().wait_recv()
    offsets[...] = cell_in[...] >> 7
    to_scalars = pltpu.make_async_copy(offsets, offset_of, load_sem.at[len(loads)])
    to_scalars.start()

    for e, w in order:
        kappa_copy(e, w, column_mate(e, w)).wait_recv()

    def strip(j):
        window = slab[:, j * EDGE : j * EDGE + WIDE]
        passed = dot_t(window, col_high[...]) + dot_t(window, col_low[...])
        for c in range(4):
            lanes = slice(j * EDGE, (j + 1) * EDGE)
            pass_high[c, :, lanes], pass_low[c, :, lanes] = split(passed[:, c * EDGE : (c + 1) * EDGE])

    last = cols // EDGE - 1
    for j in range(1, last):
        strip(j)
    for e, w in order:
        edge_copy(e, w, column_mate(e, w)).wait_recv()
    slab[:, EDGE + cols :] = slab[:, 0:EDGE]
    strip(0)
    strip(last)
    strips = cols // 128
    flat_rows = rows_of.reshape(rows * cols // 16, 128)
    for c in range(CHANNELS):
        if c < 4:
            field = (
                dot(row_high[c], pass_high[c]) + dot(row_low[c], pass_high[c]) + dot(row_high[c], pass_low[c])
            ).astype(BF16)
        else:
            field = slab[:, EDGE : EDGE + cols]
        table[c * rows : (c + 1) * rows, :] = field
        exact = field.astype(F32)
        for j in range(strips):
            flat_rows[pl.ds(j * 8 + c, rows, stride=8 * strips), :] = exact[:, j * 128 : (j + 1) * 128]
    to_scalars.wait()

    lane = iota((8, 128), 1)
    sublane = iota((8, 128), 0)

    def place(u, slot):
        kk, t = peer(u)
        return t >> 1, (mod(t, 2) * 2 + kk) * 2 + slot

    def ids_of(u, slot):
        group, row = place(u, slot)
        return cell_in[group, pl.ds(row, 1), :]

    def by_matmul(u):
        ids = jnp.concatenate([ids_of(u, 0), ids_of(u, 1)], axis=1)
        hot = (iota((cols, 256), 0) == (ids & (cols - 1))).astype(F32).astype(BF16)
        picked = dot(table[...], hot)
        mine = iota((rows, 256), 0) == (ids >> 9)
        values = [
            jnp.sum(jnp.where(mine, picked[c * rows : (c + 1) * rows], 0.0), axis=0, keepdims=True)
            for c in range(CHANNELS)
        ]
        pad = [jnp.zeros((3, 128), F32)]
        return jnp.concatenate([v[:, :128] for v in values] + pad + [v[:, 128:] for v in values] + pad, axis=0)

    def by_rows(u):
        slots = []
        for slot in range(2):
            group, row = place(u, slot)
            low = jnp.broadcast_to(ids_of(u, slot) & 127, (8, 128))
            sums = [jnp.zeros((8, 128), F32) for _ in range(4)]
            for n in range(128):
                picked = jnp.take_along_axis(rows_of[offset_of[group, row, n]], low, axis=1)
                sums[n % 4] = jnp.where(lane == n, picked, sums[n % 4])
            total = (sums[0] + sums[1]) + (sums[2] + sums[3])
            slots.append(jnp.where(sublane < CHANNELS, total, 0.0))
        return jnp.concatenate(slots, axis=0)

    def found_copy(u):
        kk, t = peer(u)
        return remote(
            found.at[u], samples.at[k * tiles + r], found_send.at[0], found_recv.at[0], base + kk, t
        )

    def all_found():
        most = pl.ds(0, peers - 1)
        return remote(found.at[most], samples.at[most], found_send.at[0], found_recv.at[0], p, r)

    @pl.loop(0, peers // GROUP)
    def _(g):
        for i in range(GROUP):
            u = g * GROUP + i
            found[u] = (by_matmul if i < GROUP // 2 else by_rows)(u).astype(BF16)

        @pl.when(g > 0)
        def _():
            found_copy(g * GROUP).start()

        for i in range(1, GROUP):
            found_copy(g * GROUP + i).start()

    samples[k * tiles + r] = found[0]
    all_found().wait_recv()

    initial = (start_xy[0], start_xy[1], 1.0, 0.0, 0.0, 1.0)
    state = (start_xy[0], start_xy[1]) + tuple(
        jnp.full((blocks, 128), v, F32) for v in initial[2:]
    )
    for m in range(2):
        target = jnp.concatenate([target_cols[m] * 8 + c for c in range(CHANNELS)], axis=0)
        wanted = (iota((CHANNELS * blocks, tiles * 16), 1) == target).astype(F32).astype(BF16)
        got = dot(wanted, samples[m * tiles : (m + 1) * tiles].reshape(tiles * 16, 128))
        state = advance(
            state, [got[c * blocks : (c + 1) * blocks] for c in range(CHANNELS)], LENS_WEIGHTS[m]
        )
    for v in range(6):
        value = jnp.where(traced_col, state[v], initial[v])
        ref, row = (final, v) if v < 2 else (jacobian, v - 2)
        for b in range(blocks):
            ref[row : row + 1, b * 128 : (b + 1) * 128] = value[b : b + 1]

    @pl.when(r < tiles - 1)
    def _():
        to_right().wait_send()

    @pl.when(r > 0)
    def _():
        to_left().wait_send()

    for e, w in order:
        kappa_copy(e, w, p).wait_send()
        edge_copy(e, w, p).wait_send()
    for w in range(1, 4):
        cell_near(w, False).wait_send()
    all_cells().wait_send()
    all_found().wait_send()


def local(planes, tiles, kappa, row_kernel, col_kernel, positions, cells, owners, counts):
    own_rows, cols = kappa.shape[1:]
    rows = planes * own_rows
    blocks = owners.shape[1]
    rays = positions.shape[1]
    peers = 2 * tiles
    in_vmem = pl.BlockSpec(memory_space=pltpu.VMEM)
    in_hbm = pl.BlockSpec(memory_space=pltpu.HBM)
    dma = pltpu.SemaphoreType.DMA
    vmem = pltpu.VMEM
    ints = jnp.int32
    return pl.pallas_call(
        functools.partial(kernel, planes, tiles),
        out_shape=(
            jax.ShapeDtypeStruct((2, rays), F32),
            jax.ShapeDtypeStruct((4, rays), F32),
        ),
        in_specs=[in_hbm] * 7,
        out_specs=(in_vmem, in_vmem),
        scratch_shapes=[
            vmem(row_kernel.shape, F32),
            vmem(col_kernel.shape, F32),
            vmem(positions.shape, F32),
            vmem(cells.shape, ints),
            vmem((2, 1, blocks), ints),
            pltpu.SMEM(counts.shape, ints),
            vmem((rows, cols + 2 * EDGE), BF16),
            vmem((2, 2, own_rows, EDGE), BF16),
            vmem((2, own_rows, EDGE), BF16),
            vmem((8, WIDE), F32),
            vmem((4 * EDGE, WIDE), BF16),
            vmem((4 * EDGE, WIDE), BF16),
            vmem((4, rows, rows), BF16),
            vmem((4, rows, rows), BF16),
            vmem((4, rows, cols), BF16),
            vmem((4, rows, cols), BF16),
            vmem((CHANNELS * rows, cols), BF16),
            vmem((rows * cols // 128, 8, 128), F32),
            vmem((2, blocks, 128), F32),
            vmem((2, blocks, 128), ints),
            vmem((4, tiles, 128), ints),
            vmem((4, tiles, 128), ints),
            vmem((tiles // 2, 8, 128), ints),
            vmem((tiles // 2, 8, 128), ints),
            vmem((tiles // 2, 8, 128), ints),
            pltpu.SMEM((tiles // 2, 8, 128), ints),
            vmem((peers, 16, 128), BF16),
            vmem((peers, 16, 128), BF16),
            dma((8,)),
            dma((2,)),
            dma((2,)),
            dma((planes // 2, 2)),
            dma((planes,)),
            dma((planes // 2, 2)),
            dma((planes,)),
            dma((4,)),
            dma((4,)),
            dma((1,)),
            dma((1,)),
            dma((1,)),
            dma((1,)),
        ],
        compiler_params=pltpu.CompilerParams(
            collective_id=0, has_side_effects=True, vmem_limit_bytes=60 * 2**20
        ),
    )(kappa, row_kernel, col_kernel, positions, cells, owners.reshape(2, 1, blocks), counts)


def solution(mesh):
    return jax.shard_map(
        functools.partial(local, mesh.shape["plane"], mesh.shape["ray"]),
        mesh=mesh,
        in_specs=(
            P(None, "plane", "ray"),
            P(),
            P(),
            P(None, ("plane", "ray")),
            P(None, ("plane", "ray")),
            P(None, ("plane", "ray"), None),
            P(("plane", "ray")),
        ),
        out_specs=(P(None, ("plane", "ray")), P(None, ("plane", "ray"))),
        check_vma=False,
    )
```

```python
import functools
import jax
import jax.numpy as jnp
from jax import lax
from jax.experimental import pallas as pl
from jax.experimental.pallas import tpu as pltpu
from jax.sharding import PartitionSpec as P

MESH = pl.DeviceIdType.MESH
LENS_WEIGHTS = (0.6, 0.4)
CHANNELS = 5
EDGE = 128
WIDE = 384
GROUP = 16
BY_MATMUL = 7
F32 = jnp.float32
BF16 = jnp.bfloat16


def iota(shape, dim):
    return lax.broadcasted_iota(jnp.int32, shape, dim)


def mod(a, b):
    return a & (b - 1)


def split(x):
    high = x.astype(BF16)
    return high, (x - high.astype(F32)).astype(BF16)


def dot(a, b):
    return jnp.dot(a, b, preferred_element_type=F32)


def dot_t(a, b):
    return lax.dot_general(a, b, (((1,), (1,)), ((), ())), preferred_element_type=F32)


def advance(ray_state, samples, plane_weight):
    pos_x, pos_y, jac_xx, jac_xy, jac_yx, jac_yy = ray_state
    deflect_x, deflect_y, shear_one, shear_two, converge = samples
    mat_xx = converge + shear_one
    mat_yy = converge - shear_one
    return (
        pos_x - plane_weight * deflect_x,
        pos_y - plane_weight * deflect_y,
        jac_xx - plane_weight * (mat_xx * jac_xx + shear_two * jac_yx),
        jac_xy - plane_weight * (mat_xx * jac_xy + shear_two * jac_yy),
        jac_yx - plane_weight * (shear_two * jac_xx + mat_yy * jac_yx),
        jac_yy - plane_weight * (shear_two * jac_xy + mat_yy * jac_yy),
    )


def kernel(
    planes, tiles,
    kappa_hbm, row_kernel_hbm, col_kernel_hbm, positions_hbm, cells_hbm, owners_hbm, counts_hbm,
    final, jacobian,
    row_kernel, col_kernel, positions, cells, owners, counts,
    slab, halo, edge, taps, col_high, col_low, row_high, row_low, pass_high, pass_low, table, rows_of,
    start_xy, cell_rows, cell_out, cell_one, cell_mid, cell_in, offsets, offset_of, found, samples,
    load_sem, halo_send, halo_recv, kappa_send, kappa_recv, edge_send, edge_recv,
    near_send, near_recv, cell_send, cell_recv, found_send, found_recv,
):
    groups = tiles // 2
    p, r = lax.axis_index("plane"), lax.axis_index("ray")
    k = mod(p, 2)
    base = p - k
    home, zl = r >> 1, mod(r, 2)
    near = zl * 2 + k
    own_rows, cols = kappa_hbm.shape[1:]
    rows = planes * own_rows
    blocks = owners.shape[2]
    peers = 2 * tiles
    margin = (row_kernel.shape[1] - 1) // 2

    def peer(u):
        return mod(k + u, 2), mod(r + (u >> 1), tiles)

    def near_mate(w):
        q = mod(near + w, 4)
        return q, base + mod(q, 2), r - zl + (q >> 1)

    def group_mate(w):
        other = mod(home + w, groups)
        return other, r + 2 * (other - home)

    def column_mate(e, w):
        return mod(base + 2 * e, planes) + mod(k + w, 2)

    half = planes // 2
    order = [
        (e, w) for e in sorted(range(half), key=lambda e: -min(e, half - e)) for w in (1, 0) if (e, w) != (0, 0)
    ]
    far = [(e, w) for e, w in order if e]

    loads = [
        pltpu.make_async_copy(src, dst, load_sem.at[i])
        for i, (src, dst) in enumerate([
            (owners_hbm, owners),
            (cells_hbm, cells),
            (counts_hbm, counts),
            (row_kernel_hbm, row_kernel),
            (col_kernel_hbm, col_kernel),
            (positions_hbm, positions),
            (kappa_hbm.at[k], slab.at[pl.ds(p * own_rows, own_rows), pl.ds(EDGE, cols)]),
        ])
    ]
    for load in loads[:3]:
        load.start()

    barrier = pltpu.get_barrier_semaphore()

    def greet(dp, dr):
        pl.semaphore_signal(barrier, inc=1, device_id=(dp, dr), device_id_type=MESH)

    @pl.when(r > 0)
    def _():
        greet(p, r - 1)

    @pl.when(r < tiles - 1)
    def _():
        greet(p, r + 1)

    for w in range(1, 4):
        greet(*near_mate(w)[1:])
    for e, w in far:
        greet(column_mate(e, w), r)
    for w in range(1, groups):
        greet(p, group_mate(w)[1])

    for load in loads[:3]:
        load.wait()

    for b in range(blocks):
        lanes = pl.ds(b * 128, 128)
        for m in range(2):
            cell_rows[m, b : b + 1, :] = cells[m : m + 1, lanes]
    left_id = iota((blocks, blocks), 0)
    right_id = iota((blocks, blocks), 1)
    traced_row = iota((1, blocks), 1) < counts[0]
    traced_col = iota((blocks, 1), 0) < counts[0]
    target_cols = []
    for m in range(2):
        owner_row = owners[m]
        owner_col = jnp.sum(
            jnp.where(left_id == right_id, jnp.broadcast_to(owner_row, (blocks, blocks)), 0),
            axis=1, keepdims=True,
        )
        same = owner_col == owner_row
        slot_row = jnp.sum((same & (left_id < right_id)).astype(jnp.int32), axis=0, keepdims=True)
        slot_col = jnp.sum((same & (right_id < left_id)).astype(jnp.int32), axis=1, keepdims=True)
        dest_row = jnp.where(
            traced_row, (owner_row & 1) * tiles + (owner_row >> 1) * 2 + slot_row, -1
        )
        target_cols.append(jnp.where(traced_col, owner_col * 2 + slot_col, -1))
        choose = (iota((peers, blocks), 0) == dest_row).astype(jnp.int32)
        ids = cell_rows[m]
        out = sum(choose[:, b : b + 1] * ids[b : b + 1] for b in range(blocks))
        for z in range(2):
            cell_out[z * 2 + m] = out[z * tiles : (z + 1) * tiles]

    sides = jnp.minimum(r, 1) + jnp.minimum(tiles - 1 - r, 1)
    pl.semaphore_wait(barrier, 3 + len(far) + groups - 1 + sides)

    def remote(src, dst, send_sem, recv_sem, dp, dr):
        return pltpu.make_async_remote_copy(
            src_ref=src, dst_ref=dst, send_sem=send_sem, recv_sem=recv_sem,
            device_id=(dp, dr), device_id_type=MESH,
        )

    def to_right():
        return remote(
            kappa_hbm.at[:, :, pl.ds(cols - EDGE, EDGE)], halo.at[0], halo_send.at[0], halo_recv.at[0], p, r + 1
        )

    def to_left():
        return remote(
            kappa_hbm.at[:, :, pl.ds(0, EDGE)], halo.at[1], halo_send.at[1], halo_recv.at[1], p, r - 1
        )

    def own_part(q, lanes):
        return slab.at[pl.ds(q * own_rows, own_rows), lanes]

    def kappa_copy(e, w, sender):
        return remote(
            kappa_hbm.at[mod(k + w, 2)], own_part(sender, pl.ds(EDGE, cols)),
            kappa_send.at[e, w], kappa_recv.at[sender], column_mate(e, w), r,
        )

    def edge_copy(e, w, sender):
        return remote(
            edge.at[mod(k + w, 2)], own_part(sender, pl.ds(0, EDGE)),
            edge_send.at[e, w], edge_recv.at[sender], column_mate(e, w), r,
        )

    def cell_near(w, arrival):
        q, dp, dr = near_mate(w)
        slot = q if arrival else near
        return remote(cell_out.at[q], cell_one.at[slot], near_send.at[w], near_recv.at[slot], dp, dr)

    def cell_far(w):
        other, dr = group_mate(w)
        return remote(
            cell_mid.at[other], cell_in.at[home], cell_send.at[0], cell_recv.at[0], p, dr
        )

    def all_cells():
        most = pl.ds(0, groups - 1)
        return remote(cell_mid.at[most], cell_in.at[most], cell_send.at[0], cell_recv.at[0], p, r)

    @pl.when(r < tiles - 1)
    def _():
        to_right().start()

    @pl.when(r > 0)
    def _():
        to_left().start()

    for w in range(1, 4):
        cell_near(w, False).start()
    for e, w in order:
        kappa_copy(e, w, p).start()
    for load in loads[3:]:
        load.start()
    cell_one[near] = cell_out[near]

    @pl.when(r == 0)
    def _():
        halo[0] = jnp.zeros(halo.shape[1:], BF16)

    @pl.when(r == tiles - 1)
    def _():
        halo[1] = jnp.zeros(halo.shape[1:], BF16)

    for load in loads[3:]:
        load.wait()

    taps[...] = jnp.zeros_like(taps)
    taps[0:4, 0 : row_kernel.shape[1]] = row_kernel[...]
    taps[4:8, 0 : row_kernel.shape[1]] = col_kernel[...]

    def bands(c):
        across = jnp.broadcast_to(taps[4 + c : 5 + c, :], (EDGE, WIDE))
        band = pltpu.roll(across, EDGE - margin, 1, stride=1, stride_axis=0)
        col_high[c * EDGE : (c + 1) * EDGE, :], col_low[c * EDGE : (c + 1) * EDGE, :] = split(band)
        down = jnp.broadcast_to(taps[c : c + 1, :], (rows, WIDE))
        band = pltpu.roll(down, WIDE - margin, 1, stride=1, stride_axis=0)[:, :rows]
        row_high[c], row_low[c] = split(band)

    bands(0)

    @pl.when(r > 0)
    def _():
        to_right().wait_recv()

    @pl.when(r < tiles - 1)
    def _():
        to_left().wait_recv()

    for m in range(2):
        packed = jnp.where(
            iota((own_rows, EDGE), 1) < EDGE // 2, halo[1, m].astype(F32), halo[0, m].astype(F32)
        )
        edge[m] = packed.astype(BF16)
    for e, w in order:
        edge_copy(e, w, p).start()
    slab[pl.ds(p * own_rows, own_rows), 0:EDGE] = edge[k]

    for w in range(1, 4):
        cell_near(w, True).wait_recv()
    for q in range(4):
        for g in range(groups):
            cell_mid[g, 2 * q : 2 * q + 2, :] = cell_one[q, 2 * g : 2 * g + 2, :]
    for w in range(1, groups):
        cell_far(w).start()
    cell_in[home] = cell_mid[home]
    bands(1)
    bands(2)
    bands(3)
    for b in range(blocks):
        lanes = pl.ds(b * 128, 128)
        for m in range(2):
            start_xy[m, b : b + 1, :] = positions[m : m + 1, lanes]
    all_cells().wait_recv()
    offsets[...] = cell_in[...] >> 7
    to_scalars = pltpu.make_async_copy(offsets, offset_of, load_sem.at[len(loads)])
    to_scalars.start()

    for e, w in order:
        kappa_copy(e, w, column_mate(e, w)).wait_recv()

    def strip(j):
        window = slab[:, j * EDGE : j * EDGE + WIDE]
        passed = dot_t(window, col_high[...]) + dot_t(window, col_low[...])
        for c in range(4):
            lanes = slice(j * EDGE, (j + 1) * EDGE)
            pass_high[c, :, lanes], pass_low[c, :, lanes] = split(passed[:, c * EDGE : (c + 1) * EDGE])

    last = cols // EDGE - 1
    for j in range(1, last):
        strip(j)
    for e, w in order:
        edge_copy(e, w, column_mate(e, w)).wait_recv()
    slab[:, EDGE + cols :] = slab[:, 0:EDGE]
    strip(0)
    strip(last)
    strips = cols // 128
    flat_rows = rows_of.reshape(rows * cols // 16, 128)
    for c in range(CHANNELS):
        if c < 4:
            field = (
                dot(row_high[c], pass_high[c]) + dot(row_low[c], pass_high[c]) + dot(row_high[c], pass_low[c])
            ).astype(BF16)
        else:
            field = slab[:, EDGE : EDGE + cols]
        table[c * rows : (c + 1) * rows, :] = field
        exact = field.astype(F32)
        for j in range(strips):
            flat_rows[pl.ds(j * 8 + c, rows, stride=8 * strips), :] = exact[:, j * 128 : (j + 1) * 128]
    to_scalars.wait()

    lane = iota((8, 128), 1)
    sublane = iota((8, 128), 0)

    def place(u, slot):
        kk, t = peer(u)
        return t >> 1, (mod(t, 2) * 2 + kk) * 2 + slot

    def ids_of(u, slot):
        group, row = place(u, slot)
        return cell_in[group, pl.ds(row, 1), :]

    def by_matmul(u):
        ids = jnp.concatenate([ids_of(u, 0), ids_of(u, 1)], axis=1)
        hot = (iota((cols, 256), 0) == (ids & (cols - 1))).astype(F32).astype(BF16)
        picked = dot(table[...], hot)
        mine = iota((rows, 256), 0) == (ids >> 9)
        values = [
            jnp.sum(jnp.where(mine, picked[c * rows : (c + 1) * rows], 0.0), axis=0, keepdims=True)
            for c in range(CHANNELS)
        ]
        pad = [jnp.zeros((3, 128), F32)]
        return jnp.concatenate([v[:, :128] for v in values] + pad + [v[:, 128:] for v in values] + pad, axis=0)

    def by_rows(u):
        slots = []
        for slot in range(2):
            group, row = place(u, slot)
            low = jnp.broadcast_to(ids_of(u, slot) & 127, (8, 128))
            sums = [jnp.zeros((8, 128), F32) for _ in range(4)]
            for n in range(128):
                picked = jnp.take_along_axis(rows_of[offset_of[group, row, n]], low, axis=1)
                sums[n % 4] = jnp.where(lane == n, picked, sums[n % 4])
            total = (sums[0] + sums[1]) + (sums[2] + sums[3])
            slots.append(jnp.where(sublane < CHANNELS, total, 0.0))
        return jnp.concatenate(slots, axis=0)

    def found_copy(u):
        kk, t = peer(u)
        return remote(
            found.at[u], samples.at[k * tiles + r], found_send.at[0], found_recv.at[0], base + kk, t
        )

    def all_found():
        most = pl.ds(0, peers - 1)
        return remote(found.at[most], samples.at[most], found_send.at[0], found_recv.at[0], p, r)

    @pl.loop(0, peers // GROUP)
    def _(g):
        for i in range(GROUP):
            u = g * GROUP + i
            found[u] = (by_matmul if i < BY_MATMUL else by_rows)(u).astype(BF16)

        @pl.when(g > 0)
        def _():
            found_copy(g * GROUP).start()

        for i in range(1, GROUP):
            found_copy(g * GROUP + i).start()

    samples[k * tiles + r] = found[0]
    all_found().wait_recv()

    initial = (start_xy[0], start_xy[1], 1.0, 0.0, 0.0, 1.0)
    state = (start_xy[0], start_xy[1]) + tuple(
        jnp.full((blocks, 128), v, F32) for v in initial[2:]
    )
    for m in range(2):
        target = jnp.concatenate([target_cols[m] * 8 + c for c in range(CHANNELS)], axis=0)
        wanted = (iota((CHANNELS * blocks, tiles * 16), 1) == target).astype(F32).astype(BF16)
        got = dot(wanted, samples[m * tiles : (m + 1) * tiles].reshape(tiles * 16, 128))
        state = advance(
            state, [got[c * blocks : (c + 1) * blocks] for c in range(CHANNELS)], LENS_WEIGHTS[m]
        )
    for v in range(6):
        value = jnp.where(traced_col, state[v], initial[v])
        ref, row = (final, v) if v < 2 else (jacobian, v - 2)
        for b in range(blocks):
            ref[row : row + 1, b * 128 : (b + 1) * 128] = value[b : b + 1]

    @pl.when(r < tiles - 1)
    def _():
        to_right().wait_send()

    @pl.when(r > 0)
    def _():
        to_left().wait_send()

    for e, w in order:
        kappa_copy(e, w, p).wait_send()
        edge_copy(e, w, p).wait_send()
    for w in range(1, 4):
        cell_near(w, False).wait_send()
    all_cells().wait_send()
    all_found().wait_send()


def local(planes, tiles, kappa, row_kernel, col_kernel, positions, cells, owners, counts):
    own_rows, cols = kappa.shape[1:]
    rows = planes * own_rows
    blocks = owners.shape[1]
    rays = positions.shape[1]
    peers = 2 * tiles
    in_vmem = pl.BlockSpec(memory_space=pltpu.VMEM)
    in_hbm = pl.BlockSpec(memory_space=pltpu.HBM)
    dma = pltpu.SemaphoreType.DMA
    vmem = pltpu.VMEM
    ints = jnp.int32
    return pl.pallas_call(
        functools.partial(kernel, planes, tiles),
        out_shape=(
            jax.ShapeDtypeStruct((2, rays), F32),
            jax.ShapeDtypeStruct((4, rays), F32),
        ),
        in_specs=[in_hbm] * 7,
        out_specs=(in_vmem, in_vmem),
        scratch_shapes=[
            vmem(row_kernel.shape, F32),
            vmem(col_kernel.shape, F32),
            vmem(positions.shape, F32),
            vmem(cells.shape, ints),
            vmem((2, 1, blocks), ints),
            pltpu.SMEM(counts.shape, ints),
            vmem((rows, cols + 2 * EDGE), BF16),
            vmem((2, 2, own_rows, EDGE), BF16),
            vmem((2, own_rows, EDGE), BF16),
            vmem((8, WIDE), F32),
            vmem((4 * EDGE, WIDE), BF16),
            vmem((4 * EDGE, WIDE), BF16),
            vmem((4, rows, rows), BF16),
            vmem((4, rows, rows), BF16),
            vmem((4, rows, cols), BF16),
            vmem((4, rows, cols), BF16),
            vmem((CHANNELS * rows, cols), BF16),
            vmem((rows * cols // 128, 8, 128), F32),
            vmem((2, blocks, 128), F32),
            vmem((2, blocks, 128), ints),
            vmem((4, tiles, 128), ints),
            vmem((4, tiles, 128), ints),
            vmem((tiles // 2, 8, 128), ints),
            vmem((tiles // 2, 8, 128), ints),
            vmem((tiles // 2, 8, 128), ints),
            pltpu.SMEM((tiles // 2, 8, 128), ints),
            vmem((peers, 16, 128), BF16),
            vmem((peers, 16, 128), BF16),
            dma((8,)),
            dma((2,)),
            dma((2,)),
            dma((planes // 2, 2)),
            dma((planes,)),
            dma((planes // 2, 2)),
            dma((planes,)),
            dma((4,)),
            dma((4,)),
            dma((1,)),
            dma((1,)),
            dma((1,)),
            dma((1,)),
        ],
        compiler_params=pltpu.CompilerParams(
            collective_id=0, has_side_effects=True, vmem_limit_bytes=60 * 2**20
        ),
    )(kappa, row_kernel, col_kernel, positions, cells, owners.reshape(2, 1, blocks), counts)


def solution(mesh):
    return jax.shard_map(
        functools.partial(local, mesh.shape["plane"], mesh.shape["ray"]),
        mesh=mesh,
        in_specs=(
            P(None, "plane", "ray"),
            P(),
            P(),
            P(None, ("plane", "ray")),
            P(None, ("plane", "ray")),
            P(None, ("plane", "ray"), None),
            P(("plane", "ray")),
        ),
        out_specs=(P(None, ("plane", "ray")), P(None, ("plane", "ray"))),
        check_vma=False,
    )
```

```python
import functools
import jax
import jax.numpy as jnp
from jax import lax
from jax.experimental import pallas as pl
from jax.experimental.pallas import tpu as pltpu
from jax.sharding import PartitionSpec as P

MESH = pl.DeviceIdType.MESH
LENS_WEIGHTS = (0.6, 0.4)
CHANNELS = 5
EDGE = 128
WIDE = 384
GROUP = 16
BY_MATMUL = 7
F32 = jnp.float32
BF16 = jnp.bfloat16


def iota(shape, dim):
    return lax.broadcasted_iota(jnp.int32, shape, dim)


def mod(a, b):
    return a & (b - 1)


def split(x):
    high = x.astype(BF16)
    return high, (x - high.astype(F32)).astype(BF16)


def dot(a, b):
    return jnp.dot(a, b, preferred_element_type=F32)


def dot_t(a, b):
    return lax.dot_general(a, b, (((1,), (1,)), ((), ())), preferred_element_type=F32)


def advance(ray_state, samples, plane_weight):
    pos_x, pos_y, jac_xx, jac_xy, jac_yx, jac_yy = ray_state
    deflect_x, deflect_y, shear_one, shear_two, converge = samples
    mat_xx = converge + shear_one
    mat_yy = converge - shear_one
    return (
        pos_x - plane_weight * deflect_x,
        pos_y - plane_weight * deflect_y,
        jac_xx - plane_weight * (mat_xx * jac_xx + shear_two * jac_yx),
        jac_xy - plane_weight * (mat_xx * jac_xy + shear_two * jac_yy),
        jac_yx - plane_weight * (shear_two * jac_xx + mat_yy * jac_yx),
        jac_yy - plane_weight * (shear_two * jac_xy + mat_yy * jac_yy),
    )


def kernel(
    planes, tiles,
    kappa_hbm, row_kernel_hbm, col_kernel_hbm, positions_hbm, cells_hbm, owners_hbm, counts_hbm,
    final, jacobian,
    row_kernel, col_kernel, positions, cells, owners, counts,
    slab, halo, edge, taps, col_high, col_low, row_high, row_low, pass_high, pass_low, table, rows_of,
    start_xy, cell_rows, cell_out, cell_one, cell_mid, cell_in, offsets, offset_of, found, samples,
    load_sem, halo_send, halo_recv, kappa_send, kappa_recv, edge_send, edge_recv,
    near_send, near_recv, cell_send, cell_recv, found_send, found_recv,
):
    groups = tiles // 2
    p, r = lax.axis_index("plane"), lax.axis_index("ray")
    k = mod(p, 2)
    base = p - k
    home, zl = r >> 1, mod(r, 2)
    near = zl * 2 + k
    own_rows, cols = kappa_hbm.shape[1:]
    rows = planes * own_rows
    blocks = owners.shape[2]
    peers = 2 * tiles
    margin = (row_kernel.shape[1] - 1) // 2

    def peer(u):
        return mod(k + u, 2), mod(r + (u >> 1), tiles)

    def near_mate(w):
        q = mod(near + w, 4)
        return q, base + mod(q, 2), r - zl + (q >> 1)

    def group_mate(w):
        other = mod(home + w, groups)
        return other, r + 2 * (other - home)

    def column_mate(e, w):
        return mod(base + 2 * e, planes) + mod(k + w, 2)

    half = planes // 2
    order = [
        (e, w) for e in sorted(range(half), key=lambda e: -min(e, half - e)) for w in (1, 0) if (e, w) != (0, 0)
    ]
    far = [(e, w) for e, w in order if e]

    loads = [
        pltpu.make_async_copy(src, dst, load_sem.at[i])
        for i, (src, dst) in enumerate([
            (owners_hbm, owners),
            (cells_hbm, cells),
            (counts_hbm, counts),
            (row_kernel_hbm, row_kernel),
            (col_kernel_hbm, col_kernel),
            (positions_hbm, positions),
            (kappa_hbm.at[k], slab.at[pl.ds(p * own_rows, own_rows), pl.ds(EDGE, cols)]),
        ])
    ]
    for load in loads[:3]:
        load.start()

    barrier = pltpu.get_barrier_semaphore()

    def greet(dp, dr):
        pl.semaphore_signal(barrier, inc=1, device_id=(dp, dr), device_id_type=MESH)

    @pl.when(r > 0)
    def _():
        greet(p, r - 1)

    @pl.when(r < tiles - 1)
    def _():
        greet(p, r + 1)

    for w in range(1, 4):
        greet(*near_mate(w)[1:])
    for e, w in far:
        greet(column_mate(e, w), r)
    for w in range(1, groups):
        greet(p, group_mate(w)[1])

    for load in loads[:3]:
        load.wait()

    for b in range(blocks):
        lanes = pl.ds(b * 128, 128)
        for m in range(2):
            cell_rows[m, b : b + 1, :] = cells[m : m + 1, lanes]
    left_id = iota((blocks, blocks), 0)
    right_id = iota((blocks, blocks), 1)
    traced_row = iota((1, blocks), 1) < counts[0]
    traced_col = iota((blocks, 1), 0) < counts[0]
    target_cols = []
    for m in range(2):
        owner_row = owners[m]
        owner_col = jnp.sum(
            jnp.where(left_id == right_id, jnp.broadcast_to(owner_row, (blocks, blocks)), 0),
            axis=1, keepdims=True,
        )
        same = owner_col == owner_row
        slot_row = jnp.sum((same & (left_id < right_id)).astype(jnp.int32), axis=0, keepdims=True)
        slot_col = jnp.sum((same & (right_id < left_id)).astype(jnp.int32), axis=1, keepdims=True)
        dest_row = jnp.where(
            traced_row, (owner_row & 1) * tiles + (owner_row >> 1) * 2 + slot_row, -1
        )
        target_cols.append(jnp.where(traced_col, owner_col * 2 + slot_col, -1))
        choose = (iota((peers, blocks), 0) == dest_row).astype(jnp.int32)
        ids = cell_rows[m]
        out = sum(choose[:, b : b + 1] * ids[b : b + 1] for b in range(blocks))
        for z in range(2):
            cell_out[z * 2 + m] = out[z * tiles : (z + 1) * tiles]

    sides = jnp.minimum(r, 1) + jnp.minimum(tiles - 1 - r, 1)
    pl.semaphore_wait(barrier, 3 + len(far) + groups - 1 + sides)

    def remote(src, dst, send_sem, recv_sem, dp, dr):
        return pltpu.make_async_remote_copy(
            src_ref=src, dst_ref=dst, send_sem=send_sem, recv_sem=recv_sem,
            device_id=(dp, dr), device_id_type=MESH,
        )

    def to_right():
        return remote(
            kappa_hbm.at[:, :, pl.ds(cols - EDGE, EDGE)], halo.at[0], halo_send.at[0], halo_recv.at[0], p, r + 1
        )

    def to_left():
        return remote(
            kappa_hbm.at[:, :, pl.ds(0, EDGE)], halo.at[1], halo_send.at[1], halo_recv.at[1], p, r - 1
        )

    def own_part(q, lanes):
        return slab.at[pl.ds(q * own_rows, own_rows), lanes]

    def kappa_copy(e, w, sender):
        return remote(
            kappa_hbm.at[mod(k + w, 2)], own_part(sender, pl.ds(EDGE, cols)),
            kappa_send.at[e, w], kappa_recv.at[sender], column_mate(e, w), r,
        )

    def edge_copy(e, w, sender):
        return remote(
            edge.at[mod(k + w, 2)], own_part(sender, pl.ds(0, EDGE)),
            edge_send.at[e, w], edge_recv.at[sender], column_mate(e, w), r,
        )

    def cell_near(w, arrival):
        q, dp, dr = near_mate(w)
        slot = q if arrival else near
        return remote(cell_out.at[q], cell_one.at[slot], near_send.at[w], near_recv.at[slot], dp, dr)

    def cell_far(w):
        other, dr = group_mate(w)
        return remote(
            cell_mid.at[other], cell_in.at[home], cell_send.at[0], cell_recv.at[0], p, dr
        )

    def all_cells():
        most = pl.ds(0, groups - 1)
        return remote(cell_mid.at[most], cell_in.at[most], cell_send.at[0], cell_recv.at[0], p, r)

    @pl.when(r < tiles - 1)
    def _():
        to_right().start()

    @pl.when(r > 0)
    def _():
        to_left().start()

    for w in range(1, 4):
        cell_near(w, False).start()
    for e, w in order:
        kappa_copy(e, w, p).start()
    for load in loads[3:]:
        load.start()
    cell_one[near] = cell_out[near]

    @pl.when(r == 0)
    def _():
        halo[0] = jnp.zeros(halo.shape[1:], BF16)

    @pl.when(r == tiles - 1)
    def _():
        halo[1] = jnp.zeros(halo.shape[1:], BF16)

    for load in loads[3:]:
        load.wait()

    taps[...] = jnp.zeros_like(taps)
    taps[0:4, 0 : row_kernel.shape[1]] = row_kernel[...]
    taps[4:8, 0 : row_kernel.shape[1]] = col_kernel[...]

    def bands(c):
        across = jnp.broadcast_to(taps[4 + c : 5 + c, :], (EDGE, WIDE))
        band = pltpu.roll(across, EDGE - margin, 1, stride=1, stride_axis=0)
        col_high[c * EDGE : (c + 1) * EDGE, :], col_low[c * EDGE : (c + 1) * EDGE, :] = split(band)
        down = jnp.broadcast_to(taps[c : c + 1, :], (rows, WIDE))
        band = pltpu.roll(down, WIDE - margin, 1, stride=1, stride_axis=0)[:, :rows]
        row_high[c], row_low[c] = split(band)

    bands(0)

    @pl.when(r > 0)
    def _():
        to_right().wait_recv()

    @pl.when(r < tiles - 1)
    def _():
        to_left().wait_recv()

    for m in range(2):
        packed = jnp.where(
            iota((own_rows, EDGE), 1) < EDGE // 2, halo[1, m].astype(F32), halo[0, m].astype(F32)
        )
        edge[m] = packed.astype(BF16)
    for e, w in order:
        edge_copy(e, w, p).start()
    slab[pl.ds(p * own_rows, own_rows), 0:EDGE] = edge[k]

    for w in range(1, 4):
        cell_near(w, True).wait_recv()
    for q in range(4):
        for g in range(groups):
            cell_mid[g, 2 * q : 2 * q + 2, :] = cell_one[q, 2 * g : 2 * g + 2, :]
    for w in range(1, groups):
        cell_far(w).start()
    cell_in[home] = cell_mid[home]
    bands(1)
    bands(2)
    bands(3)
    for b in range(blocks):
        lanes = pl.ds(b * 128, 128)
        for m in range(2):
            start_xy[m, b : b + 1, :] = positions[m : m + 1, lanes]
    all_cells().wait_recv()
    offsets[...] = cell_in[...] >> 7
    to_scalars = pltpu.make_async_copy(offsets, offset_of, load_sem.at[len(loads)])
    to_scalars.start()

    for e, w in order:
        kappa_copy(e, w, column_mate(e, w)).wait_recv()

    def strip(j):
        window = slab[:, j * EDGE : j * EDGE + WIDE]
        passed = dot_t(window, col_high[...]) + dot_t(window, col_low[...])
        for c in range(4):
            lanes = slice(j * EDGE, (j + 1) * EDGE)
            pass_high[c, :, lanes], pass_low[c, :, lanes] = split(passed[:, c * EDGE : (c + 1) * EDGE])

    last = cols // EDGE - 1
    for j in range(1, last):
        strip(j)
    for e, w in order:
        edge_copy(e, w, column_mate(e, w)).wait_recv()
    slab[:, EDGE + cols :] = slab[:, 0:EDGE]
    strip(0)
    strip(last)
    strips = cols // 128
    flat_rows = rows_of.reshape(rows * cols // 16, 128)
    for c in range(CHANNELS):
        if c < 4:
            field = (
                dot(row_high[c], pass_high[c]) + dot(row_low[c], pass_high[c]) + dot(row_high[c], pass_low[c])
            ).astype(BF16)
        else:
            field = slab[:, EDGE : EDGE + cols]
        table[c * rows : (c + 1) * rows, :] = field
        exact = field.astype(F32)
        for j in range(strips):
            flat_rows[pl.ds(j * 8 + c, rows, stride=8 * strips), :] = exact[:, j * 128 : (j + 1) * 128]
    to_scalars.wait()

    lane = iota((8, 128), 1)
    sublane = iota((8, 128), 0)

    def place(u, slot):
        kk, t = peer(u)
        return t >> 1, (mod(t, 2) * 2 + kk) * 2 + slot

    def ids_of(u, slot):
        group, row = place(u, slot)
        return cell_in[group, pl.ds(row, 1), :]

    def by_matmul(u):
        ids = jnp.concatenate([ids_of(u, 0), ids_of(u, 1)], axis=1)
        hot = (iota((cols, 256), 0) == (ids & (cols - 1))).astype(F32).astype(BF16)
        picked = dot(table[...], hot)
        mine = iota((rows, 256), 0) == (ids >> 9)
        values = [
            jnp.sum(jnp.where(mine, picked[c * rows : (c + 1) * rows], 0.0), axis=0, keepdims=True)
            for c in range(CHANNELS)
        ]
        pad = [jnp.zeros((3, 128), F32)]
        return jnp.concatenate([v[:, :128] for v in values] + pad + [v[:, 128:] for v in values] + pad, axis=0)

    def by_rows(u):
        slots = []
        for slot in range(2):
            group, row = place(u, slot)
            low = jnp.broadcast_to(ids_of(u, slot) & 127, (8, 128))
            sums = [jnp.zeros((8, 128), F32) for _ in range(4)]
            for n in range(128):
                picked = jnp.take_along_axis(rows_of[offset_of[group, row, n]], low, axis=1)
                sums[n % 4] = jnp.where(lane == n, picked, sums[n % 4])
            total = (sums[0] + sums[1]) + (sums[2] + sums[3])
            slots.append(jnp.where(sublane < CHANNELS, total, 0.0))
        return jnp.concatenate(slots, axis=0)

    def found_copy(u):
        kk, t = peer(u)
        return remote(
            found.at[u], samples.at[k * tiles + r], found_send.at[0], found_recv.at[0], base + kk, t
        )

    def all_found():
        most = pl.ds(0, peers - 1)
        return remote(found.at[most], samples.at[most], found_send.at[0], found_recv.at[0], p, r)

    @pl.loop(0, peers // GROUP)
    def _(g):
        for i in range(GROUP):
            u = g * GROUP + i
            found[u] = (by_matmul if i % 2 and i < 2 * BY_MATMUL else by_rows)(u).astype(BF16)

        @pl.when(g > 0)
        def _():
            found_copy(g * GROUP).start()

        for i in range(1, GROUP):
            found_copy(g * GROUP + i).start()

    samples[k * tiles + r] = found[0]
    @pl.when(r < tiles - 1)
    def _():
        to_right().wait_send()

    @pl.when(r > 0)
    def _():
        to_left().wait_send()

    for e, w in order:
        kappa_copy(e, w, p).wait_send()
        edge_copy(e, w, p).wait_send()
    for w in range(1, 4):
        cell_near(w, False).wait_send()
    all_cells().wait_send()
    all_found().wait_recv()

    initial = (start_xy[0], start_xy[1], 1.0, 0.0, 0.0, 1.0)
    state = (start_xy[0], start_xy[1]) + tuple(
        jnp.full((blocks, 128), v, F32) for v in initial[2:]
    )
    for m in range(2):
        target = jnp.concatenate([target_cols[m] * 8 + c for c in range(CHANNELS)], axis=0)
        wanted = (iota((CHANNELS * blocks, tiles * 16), 1) == target).astype(F32).astype(BF16)
        got = dot(wanted, samples[m * tiles : (m + 1) * tiles].reshape(tiles * 16, 128))
        state = advance(
            state, [got[c * blocks : (c + 1) * blocks] for c in range(CHANNELS)], LENS_WEIGHTS[m]
        )
    for v in range(6):
        value = jnp.where(traced_col, state[v], initial[v])
        ref, row = (final, v) if v < 2 else (jacobian, v - 2)
        for b in range(blocks):
            ref[row : row + 1, b * 128 : (b + 1) * 128] = value[b : b + 1]

    all_found().wait_send()


def local(planes, tiles, kappa, row_kernel, col_kernel, positions, cells, owners, counts):
    own_rows, cols = kappa.shape[1:]
    rows = planes * own_rows
    blocks = owners.shape[1]
    rays = positions.shape[1]
    peers = 2 * tiles
    in_vmem = pl.BlockSpec(memory_space=pltpu.VMEM)
    in_hbm = pl.BlockSpec(memory_space=pltpu.HBM)
    dma = pltpu.SemaphoreType.DMA
    vmem = pltpu.VMEM
    ints = jnp.int32
    return pl.pallas_call(
        functools.partial(kernel, planes, tiles),
        out_shape=(
            jax.ShapeDtypeStruct((2, rays), F32),
            jax.ShapeDtypeStruct((4, rays), F32),
        ),
        in_specs=[in_hbm] * 7,
        out_specs=(in_vmem, in_vmem),
        scratch_shapes=[
            vmem(row_kernel.shape, F32),
            vmem(col_kernel.shape, F32),
            vmem(positions.shape, F32),
            vmem(cells.shape, ints),
            vmem((2, 1, blocks), ints),
            pltpu.SMEM(counts.shape, ints),
            vmem((rows, cols + 2 * EDGE), BF16),
            vmem((2, 2, own_rows, EDGE), BF16),
            vmem((2, own_rows, EDGE), BF16),
            vmem((8, WIDE), F32),
            vmem((4 * EDGE, WIDE), BF16),
            vmem((4 * EDGE, WIDE), BF16),
            vmem((4, rows, rows), BF16),
            vmem((4, rows, rows), BF16),
            vmem((4, rows, cols), BF16),
            vmem((4, rows, cols), BF16),
            vmem((CHANNELS * rows, cols), BF16),
            vmem((rows * cols // 128, 8, 128), F32),
            vmem((2, blocks, 128), F32),
            vmem((2, blocks, 128), ints),
            vmem((4, tiles, 128), ints),
            vmem((4, tiles, 128), ints),
            vmem((tiles // 2, 8, 128), ints),
            vmem((tiles // 2, 8, 128), ints),
            vmem((tiles // 2, 8, 128), ints),
            pltpu.SMEM((tiles // 2, 8, 128), ints),
            vmem((peers, 16, 128), BF16),
            vmem((peers, 16, 128), BF16),
            dma((8,)),
            dma((2,)),
            dma((2,)),
            dma((planes // 2, 2)),
            dma((planes,)),
            dma((planes // 2, 2)),
            dma((planes,)),
            dma((4,)),
            dma((4,)),
            dma((1,)),
            dma((1,)),
            dma((1,)),
            dma((1,)),
        ],
        compiler_params=pltpu.CompilerParams(
            collective_id=0, has_side_effects=True, vmem_limit_bytes=60 * 2**20
        ),
    )(kappa, row_kernel, col_kernel, positions, cells, owners.reshape(2, 1, blocks), counts)


def solution(mesh):
    return jax.shard_map(
        functools.partial(local, mesh.shape["plane"], mesh.shape["ray"]),
        mesh=mesh,
        in_specs=(
            P(None, "plane", "ray"),
            P(),
            P(),
            P(None, ("plane", "ray")),
            P(None, ("plane", "ray")),
            P(None, ("plane", "ray"), None),
            P(("plane", "ray")),
        ),
        out_specs=(P(None, ("plane", "ray")), P(None, ("plane", "ray"))),
        check_vma=False,
    )
```
